256 devices in a mesh: dp: 2 (over y_lo), ctx: 32 (over z, y_hi, core), mp: 4 (over x).
Axes of the slice: x: 4, y: 4 (y_hi: 2, y_lo: 2; y = y_hi * 2 + y_lo), z: 8, core: 2. Of those that a mesh axis runs over, the one named last changes fastest.
Arguments:
- queries: bfloat16 [2, 4096, 2048], P('dp', 'ctx', 'mp'), may hold values from -6 to 6
- key_rows: bfloat16 [2, 4096, 2048], P('dp', 'ctx', 'mp'), may hold values from -6 to 6
- value_rows: bfloat16 [2, 4096, 2048], P('dp', 'ctx', 'mp'), may hold values from -6 to 6
- out_weight: bfloat16 [4096, 2048], P(('dp', 'ctx'), 'mp'), may hold values from -0.125 to 0.125
- out_grad: bfloat16 [2, 4096, 4096], P('dp', 'ctx', 'mp'), may hold values from -1.5 to 1.5
- block_offsets: int32 [2, 32], P('dp'), may hold values from 0 to 31, each once within a row
Outputs:
- projected: bfloat16 [2, 4096, 4096], P('dp', 'ctx', 'mp')
- query_grad: bfloat16 [2, 4096, 2048], P('dp', 'ctx', 'mp')
- key_grad: bfloat16 [2, 4096, 2048], P('dp', 'ctx', 'mp')
- value_grad: bfloat16 [2, 4096, 2048], P('dp', 'ctx', 'mp')
- weight_grad: float32 [4096, 2048], P(('dp', 'ctx'), 'mp')
The draws below stay inside these ranges and needn't reach their ends.
Inputs may be any that keep to these rules, and one draw needn't show every extreme that they name: Each row of block_offsets is a permutation of 0 to 31.
All inputs are finite; a program needn't handle non-finite values.
Results may differ from the reference program's by a relative error of at most 0.04.
Values may be sent and summed in bfloat16 or wider, within the bound.
A program may use at most 128 MiB of HBM per device.

```python
import jax
import jax.numpy as jnp
from jax import lax

D = 4096
HD = 128
HEADS = 16
TOK_DEV = 128
SEQS = 2
BLOCKS = 32
SEQ = 4096
HW = 2048
N_MP = 4


def normal_rows(key):
    return jnp.clip(jax.random.normal(key, (SEQS, SEQ, HEADS * HD), jnp.float32), -6.0, 6.0)


def draw_queries(key, part):
    key = jax.random.fold_in(key, 1)
    drawn = normal_rows(key)
    return drawn.astype(jnp.bfloat16)


def draw_key_rows(key, part):
    key = jax.random.fold_in(key, 2)
    drawn = normal_rows(key)
    return drawn.astype(jnp.bfloat16)


def levels(own_key, extent, split, low, largest):
    gain = 1.0
    for dim, parts in split:
        draws = jax.random.uniform(jax.random.fold_in(jax.random.fold_in(own_key, 6), dim), (parts,), jnp.float32, low / len(split), largest / len(split))
        gain = gain * jnp.repeat(jnp.exp(draws), extent[dim] // parts).reshape((-1,) + (1,) * (len(extent) - 1 - dim))
    return gain


def normal_values(stream_key, shape, deviation, reach, cuts=(), held_as=jnp.bfloat16):
    entries = deviation * jax.random.normal(stream_key, shape, jnp.float32)
    if cuts:
        entries = entries * levels(stream_key, shape, cuts, -0.22, 0.18)
    return jnp.clip(entries, -reach, reach).astype(held_as)


def setup_inputs(seed: int = 0) -> dict:
    arg_keys = jax.random.split(jax.random.key(seed), 7)
    return {
        "queries": draw_queries(jax.random.fold_in(arg_keys[6], 71), 0),
        "key_rows": draw_key_rows(jax.random.fold_in(arg_keys[6], 71), 0),
        "value_rows": normal_values(arg_keys[2], (SEQS, SEQ, HW), 1.0, 6.0, ((0, 2), (1, 32), (2, 4))),
        "out_weight": normal_values(arg_keys[3], (D, HW), HW ** -0.5, 0.125, ((0, 64), (1, 4))),
        "out_grad": normal_values(arg_keys[4], (SEQS, SEQ, D), 0.25, 1.5, ((0, 2), (1, 32), (2, 4))),
        "block_offsets": jax.vmap(lambda own: jax.random.permutation(own, BLOCKS))(jax.random.split(arg_keys[5], SEQS)).reshape((SEQS, BLOCKS)).astype(jnp.int32),
    }


MASKED = -1.0e30


def head_pass(head_items):
    q_rows, k_rows, v_rows, grad_rows, positions = head_items
    score_scale = HD ** -0.5
    allowed = positions[None, :] <= positions[:, None]
    scores = jnp.where(allowed, jnp.dot(q_rows, k_rows.T, preferred_element_type=jnp.float32) * score_scale, MASKED)
    row_top = jnp.max(scores, axis=1, keepdims=True)
    raised = jnp.where(allowed, jnp.exp(scores - row_top), 0.0)
    row_total = jnp.sum(raised, axis=1, keepdims=True)
    attended = (jnp.dot(raised.astype(jnp.bfloat16), v_rows, preferred_element_type=jnp.float32) / row_total).astype(jnp.bfloat16)
    log_total = row_top + jnp.log(row_total)
    row_delta = jnp.sum(grad_rows.astype(jnp.float32) * attended.astype(jnp.float32), axis=1, keepdims=True)
    attn_prob = jnp.where(allowed, jnp.exp(scores - log_total), 0.0)
    value_grad = jnp.dot(attn_prob.astype(jnp.bfloat16).T, grad_rows, preferred_element_type=jnp.float32)
    prob_grad = jnp.dot(grad_rows, v_rows.T, preferred_element_type=jnp.float32)
    score_grad = (attn_prob * (prob_grad - row_delta) * score_scale).astype(jnp.bfloat16)
    query_grad = jnp.dot(score_grad, k_rows, preferred_element_type=jnp.float32)
    key_grad = jnp.dot(score_grad.T, q_rows, preferred_element_type=jnp.float32)
    return attended, query_grad.astype(jnp.bfloat16), key_grad.astype(jnp.bfloat16), value_grad.astype(jnp.bfloat16)


def to_heads(values):
    return values.reshape(SEQS, SEQ, HEADS, HD).transpose(0, 2, 1, 3).reshape(SEQS * HEADS, SEQ, HD)


def from_heads(values):
    return values.reshape(SEQS, HEADS, SEQ, HD).transpose(0, 2, 1, 3).reshape(SEQS, SEQ, HEADS * HD)


def reference(queries, key_rows, value_rows, out_weight, out_grad, block_offsets):
    all_width = HEADS * HD
    flat_grad = out_grad.reshape(SEQS * SEQ, D)
    grad_heads = jnp.dot(flat_grad, out_weight, preferred_element_type=jnp.float32).astype(jnp.bfloat16)
    row_ids = jnp.arange(SEQ, dtype=jnp.int32)
    positions = block_offsets[:, row_ids // TOK_DEV].astype(jnp.int32) * TOK_DEV + row_ids % TOK_DEV
    position_items = jnp.repeat(positions, HEADS, axis=0)
    attended, query_grad, key_grad, value_grad = lax.map(
        head_pass,
        (to_heads(queries), to_heads(key_rows), to_heads(value_rows), to_heads(grad_heads), position_items))
    attended = from_heads(attended)
    flat_attn = attended.reshape(SEQS * SEQ, all_width)
    group_width = all_width // N_MP
    summed = jnp.zeros((SEQS * SEQ, D), jnp.float32)
    for group_id in range(N_MP):
        lower = group_id * group_width
        part_sum = jnp.dot(flat_attn[:, lower:lower + group_width], out_weight[:, lower:lower + group_width].T,
                           preferred_element_type=jnp.float32)
        rounded = lax.optimization_barrier(part_sum.astype(jnp.bfloat16))
        summed = summed + rounded.astype(jnp.float32)
    projected = summed.astype(jnp.bfloat16).reshape(SEQS, SEQ, D)
    weight_grad = jnp.dot(flat_grad.T, flat_attn, preferred_element_type=jnp.float32)
    return projected, from_heads(query_grad), from_heads(key_grad), from_heads(value_grad), weight_grad
```

```python
import functools

import jax
import jax.numpy as jnp
from jax import lax
from jax.experimental import pallas as pl
from jax.experimental.pallas import tpu as pltpu
from jax.sharding import PartitionSpec as P

HD = 128
MASKED = -1e30
MESH = pl.DeviceIdType.MESH
BF = jnp.bfloat16
F32 = jnp.float32
PHASES = ((-1, 1), (-2, 2), (-3, 3), (4,))


class Place:
    def __init__(self):
        self.dp = lax.axis_index("dp")
        self.ctx = lax.axis_index("ctx")
        self.mp = lax.axis_index("mp")
        self.z = self.ctx // 4
        self.j = self.ctx % 4
        self.yhi = self.j // 2
        self.core = self.j % 2
        self.y = self.yhi * 2 + self.dp

    def plane(self, off):
        return (self.z + 8 + off) % 8

    def yblock(self, off):
        y = (self.y + 4 + off) % 4
        return y % 2, y // 2

    def at_z(self, off):
        return {"ctx": self.plane(off) * 4 + self.j}

    def at_y(self, off):
        dp, yhi = self.yblock(off)
        return {"dp": dp, "ctx": self.z * 4 + yhi * 2 + self.core}

    def at_x(self, off):
        return {"mp": (self.mp + 4 + off) % 4}

    def at_j(self, off):
        return {"ctx": self.z * 4 + (self.j + 4 + off) % 4}

    def sibling(self):
        return {"ctx": self.ctx + 1 - 2 * self.core}


def greet(devices):
    barrier = pltpu.get_barrier_semaphore()
    for device in devices:
        pl.semaphore_signal(barrier, inc=1, device_id=device, device_id_type=MESH)
    pl.semaphore_wait(barrier, len(devices))


class Links:
    def __init__(self, send_sems, recv_sems):
        self.send_sems, self.recv_sems = send_sems, recv_sems
        self.slots = {}
        self.sent = []

    def slot(self, name):
        return self.slots.setdefault(name, len(self.slots))

    def copy(self, name, src, dst, device):
        i = self.slot(name)
        return pltpu.make_async_remote_copy(
            src_ref=src, dst_ref=dst, send_sem=self.send_sems.at[i],
            recv_sem=self.recv_sems.at[i], device_id=device, device_id_type=MESH)

    def send(self, name, src, dst, device):
        copy = self.copy(name, src, dst, device)
        copy.start()
        self.sent.append(copy)

    def wait(self, name, dst, device):
        self.copy(name, dst, dst, device).wait_recv()

    def drain(self):
        for copy in self.sent:
            copy.wait_send()


def gather_kernel(q, k, v, w, og, qh, kv, wf, ogf, send_sems, recv_sems, local_sems):
    at = Place()
    z, j, core = at.z, at.j, at.core
    greet([at.at_j(1), at.at_j(2), at.at_j(3), at.at_z(1), at.at_z(-1),
           at.at_y(1), at.at_y(-1), at.at_x(1), at.at_x(-1)])
    links = Links(send_sems, recv_sems)

    def head(ref, off):
        return ref.at[:, pl.ds(pl.multiple_of((j + 4 + off) % 4 * HD, HD), HD)]

    def wblock(zoff, yoff, half=None):
        dp, yhi = at.yblock(yoff)
        ref = wf.at[dp, at.plane(zoff), yhi, core]
        return ref if half is None else ref.at[pl.ds(half * 32, 32)]

    own = [
        pltpu.make_async_copy(head(k, 0), kv.at[0, z, j], local_sems.at[0]),
        pltpu.make_async_copy(head(v, 0), kv.at[1, z, j], local_sems.at[1]),
        pltpu.make_async_copy(w, wblock(0, 0), local_sems.at[2]),
        pltpu.make_async_copy(head(q, 0), qh.at[j], local_sems.at[3]),
        pltpu.make_async_copy(og, ogf.at[at.mp], local_sems.at[4]),
    ]
    for copy in own:
        copy.start()
    for a, ref in ((0, k), (1, v)):
        for t in (1, 2, 3):
            links.send(("kv", a, t), head(ref, t), kv.at[a, z, j], at.at_j(t))
    for d in (1, -1):
        links.send(("wz", d, 0), w, wblock(0, 0), at.at_z(d))
        links.send(("wy", 0, d), w, wblock(0, 0), at.at_y(d))
    for d in (1, -1):
        links.send(("og", d, 0), og, ogf.at[at.mp], at.at_x(d))
    for t in (1, 2, 3):
        links.send(("q", t), head(q, t), qh.at[j], at.at_j(t))
    own[0].wait()
    own[1].wait()
    for a in (0, 1):
        for t in (1, 2, 3):
            links.wait(("kv", a, t), kv.at[a, z, (j + 4 - t) % 4], at.at_j(t))
        for d in (1, -1):
            links.send(("z", a, d, 0), kv.at[a, z], kv.at[a, z], at.at_z(d))
    own[2].wait()

    def forward_y(off):
        for d in (1, -1):
            links.wait(("wy", off, d), wblock(off, -d), at.at_y(d))
            half = (1 - d) // 2
            links.send(("wyh", off, d), wblock(off, -d, half), wblock(off, -d, half), at.at_y(d))

    def to_sibling(off):
        for d in (1, -1):
            half = (1 - d) // 2
            links.wait(("wyh", off, d), wblock(off, 2, half), at.at_y(d))
        for dp in (0, 1):
            ref = wf.at[dp, at.plane(off), :, core]
            links.send(("sib", off, dp), ref, ref, at.sibling())

    done = (0,)
    before = ()
    for s in range(4):
        for d in (1, -1):
            if s < 3:
                links.wait(("wz", d, s), wblock(-d * (1 + s), 0), at.at_z(d))
            else:
                half = (1 - d) // 2
                links.wait(("wz", d, s), wblock(4, 0, half), at.at_z(d))
            if s < 2:
                links.send(("wz", d, s + 1), wblock(-d * (1 + s), 0), wblock(-d * (1 + s), 0), at.at_z(d))
            elif s == 2:
                half = (1 - d) // 2
                links.send(("wz", d, 3), wblock(-d * 3, 0, half), wblock(-d * 3, 0, half), at.at_z(d))
        for off in PHASES[s]:
            for d in (1, -1):
                links.send(("wy", off, d), wblock(off, 0), wblock(off, 0), at.at_y(d))
        for off in done:
            forward_y(off)
        if s == 0:
            for d in (1, -1):
                links.wait(("og", d, 0), ogf.at[(at.mp + 4 - d) % 4], at.at_x(d))
                half = ogf.at[(at.mp + 4 - d) % 4, pl.ds((1 - d) // 2 * 64, 64)]
                links.send(("og", d, 1), half, half, at.at_x(d))
        for a in (0, 1):
            for d in (1, -1):
                if s == 3 and a != (1 - d) // 2:
                    continue
                chunk = kv.at[a, at.plane(-d * (1 + s))]
                links.wait(("z", a, d, s), chunk, at.at_z(d))
                if s < 2 or (s == 2 and a == (1 - d) // 2):
                    links.send(("z", a, d, s + 1), chunk, chunk, at.at_z(d))
        for off in before:
            to_sibling(off)
        before = done
        done = PHASES[s]
    for off in done:
        forward_y(off)
    for off in before + done:
        to_sibling(off)
    for d in (1, -1):
        half = ogf.at[(at.mp + 2) % 4, pl.ds((1 - d) // 2 * 64, 64)]
        links.wait(("og", d, 1), half, at.at_x(d))
    for t in (1, 2, 3):
        links.wait(("q", t), qh.at[(j + 4 - t) % 4], at.at_j(t))
    for off in (0, -1, 1, -2, 2, -3, 3, 4):
        for dp in (0, 1):
            ref = wf.at[dp, at.plane(off), :, 1 - core]
            links.wait(("sib", off, dp), ref, at.sibling())
    own[3].wait()
    own[4].wait()
    links.drain()
    assert len(links.slots) <= 96, len(links.slots)


def any_spec(n):
    return [pl.BlockSpec(memory_space=pl.ANY)] * n


def gather(q, k, v, w, og):
    return pl.pallas_call(
        gather_kernel,
        out_shape=(
            jax.ShapeDtypeStruct((4, 128, HD), BF),
            jax.ShapeDtypeStruct((2, 8, 4, 128, HD), BF),
            jax.ShapeDtypeStruct((2, 8, 2, 2, 64, 512), BF),
            jax.ShapeDtypeStruct((4, 128, 1024), BF),
        ),
        in_specs=any_spec(5),
        out_specs=tuple(any_spec(4)),
        scratch_shapes=[
            pltpu.SemaphoreType.DMA((96,)),
            pltpu.SemaphoreType.DMA((96,)),
            pltpu.SemaphoreType.DMA((5,)),
        ],
        compiler_params=pltpu.CompilerParams(collective_id=0, has_side_effects=True),
        name="gather",
    )(q, k, v, w, og)

ORDER = (4, 3, -3, 2, -2, 1, -1, 0)
GROUPS = ((4,), (3, -3), (2, -2), (1, -1), (0,))
LOG2E = 1.4426950408889634
SCALE2 = HD ** -0.5 * LOG2E
NT = (((1,), (1,)), ((), ()))
TN = (((0,), (0,)), ((), ()))


def dot(a, b, dims=(((1,), (0,)), ((), ()))):
    return lax.dot_general(a, b, dims, preferred_element_type=F32)


def swap_kernel(gh, att, doh, att_tok, send_sems, recv_sems, local_sems):
    at = Place()
    j = at.j
    greet([at.at_j(1), at.at_j(2), at.at_j(3)])
    links = Links(send_sems, recv_sems)

    def head(ref, off):
        return ref.at[:, pl.ds(pl.multiple_of((j + 4 + off) % 4 * HD, HD), HD)]

    own = [
        pltpu.make_async_copy(head(gh, 0), doh.at[j], local_sems.at[0]),
        pltpu.make_async_copy(att.at[j], head(att_tok, 0), local_sems.at[1]),
    ]
    for t in (1, 2, 3):
        links.send(("g", t), head(gh, t), doh.at[j], at.at_j(t))
        links.send(("a", t), att.at[(j + t) % 4], head(att_tok, 0), at.at_j(t))
    for copy in own:
        copy.start()
    for t in (1, 2, 3):
        links.wait(("g", t), doh.at[(j + 4 - t) % 4], at.at_j(t))
        links.wait(("a", t), head(att_tok, -t), at.at_j(t))
    for copy in own:
        copy.wait()
    links.drain()


def swap(gh, att):
    return pl.pallas_call(
        swap_kernel,
        out_shape=(
            jax.ShapeDtypeStruct((4, 128, HD), BF),
            jax.ShapeDtypeStruct((128, 512), BF),
        ),
        in_specs=any_spec(2),
        out_specs=tuple(any_spec(2)),
        scratch_shapes=[
            pltpu.SemaphoreType.DMA((6,)),
            pltpu.SemaphoreType.DMA((6,)),
            pltpu.SemaphoreType.DMA((2,)),
        ],
        compiler_params=pltpu.CompilerParams(collective_id=1, has_side_effects=True),
        name="swap",
    )(gh, att)


def half_of(d):
    return (1 - d) // 2


def scatter_kernel(dq_h, dkv, px, wgp, dq, dk, dv, proj, wg,
                   zr, zs, zfin, xr0, xs, xr1, sibr, wsum, yr0, yr1, wy, wzr, wzs,
                   send_sems, recv_sems, local_sems):
    at = Place()
    z, j, core = at.z, at.j, at.core
    greet([at.at_j(1), at.at_j(2), at.at_j(3), at.at_z(1), at.at_z(-1),
           at.at_y(1), at.at_y(-1), at.at_x(1), at.at_x(-1)])
    links = Links(send_sems, recv_sems)

    def head(ref, off):
        return ref.at[:, pl.ds(pl.multiple_of((j + 4 + off) % 4 * HD, HD), HD)]

    def plus(*terms):
        total = terms[0].astype(F32)
        for term in terms[1:]:
            total = total + term.astype(F32)
        return total

    own = [pltpu.make_async_copy(dq_h.at[j], head(dq, 0), local_sems.at[0])]

    def zsend(s, only=None):
        for i, d in ((0, 1), (1, -1)):
            for a in (0, 1):
                if s == 0 and a != i:
                    continue
                if only is not None and only != (s == 1 and a != i):
                    continue
                p = at.plane(d * (4 - s))
                if s == 0 or (s == 1 and a != i):
                    src = dkv.at[a, p]
                else:
                    links.wait(("z", a, d, s - 1), zr.at[a, i, s - 1], at.at_z(d))
                    zs[a, i, s - 1] = plus(dkv[a, p], zr[a, i, s - 1]).astype(BF)
                    src = zs.at[a, i, s - 1]
                links.send(("z", a, d, s), src, zr.at[a, i, s], at.at_z(d))

    def zfinal():
        for a, out in ((0, dk), (1, dv)):
            for i, d in ((0, 1), (1, -1)):
                links.wait(("z", a, d, 3), zr.at[a, i, 3], at.at_z(d))
            zfin[a] = plus(dkv[a, z], zr[a, 0, 3], zr[a, 1, 3]).astype(BF)
            for t in (1, 2, 3):
                links.send(("kv", a, t), zfin.at[a, (j + t) % 4], head(out, 0), at.at_j(t))
            copy = pltpu.make_async_copy(zfin.at[a, j], head(out, 0), local_sems.at[1 + a])
            copy.start()
            own.append(copy)

    def xfirst():
        for i, d in ((0, 1), (1, -1)):
            links.send(("x", d, 0), px.at[(at.mp + 2) % 4, pl.ds(i * 64, 64)], xr0.at[i], at.at_x(d))

    def xsecond():
        for i, d in ((0, 1), (1, -1)):
            chunk = (at.mp + 4 + d) % 4
            links.wait(("x", d, 0), xr0.at[i], at.at_x(d))
            xs[i, pl.ds(i * 64, 64)] = plus(px[chunk, pl.ds(i * 64, 64)], xr0[i]).astype(BF)
            xs[i, pl.ds(64 - i * 64, 64)] = px[chunk, pl.ds(64 - i * 64, 64)]
            links.send(("x", d, 1), xs.at[i], xr1.at[i], at.at_x(d))

    def xfinal():
        for i, d in ((0, 1), (1, -1)):
            links.wait(("x", d, 1), xr1.at[i], at.at_x(d))
        proj[...] = plus(px[at.mp], xr1[0], xr1[1]).astype(BF)

    def to_sibling(off):
        for dp in (0, 1):
            p = at.plane(off)
            links.send(("sib", off, dp), wgp.at[dp, p, :, 1 - core], sibr.at[dp, p], at.sibling())

    def yfirst(off):
        p = at.plane(off)
        for dp in (0, 1):
            links.wait(("sib", off, dp), sibr.at[dp, p], at.sibling())
        for dp in (0, 1):
            for yhi in (0, 1):
                wsum[dp, p, yhi] = plus(wgp[dp, p, yhi, core], sibr[dp, p, yhi]).astype(BF)
        dp, yhi = at.yblock(2)
        for i, d in ((0, 1), (1, -1)):
            links.send(("y", off, d, 0), wsum.at[dp, p, yhi, pl.ds(i * 32, 32)], yr0.at[p, i], at.at_y(d))

    def ysecond(off):
        p = at.plane(off)
        for i, d in ((0, 1), (1, -1)):
            dp, yhi = at.yblock(d)
            links.wait(("y", off, d, 0), yr0.at[p, i], at.at_y(d))
            rows = pl.ds(i * 32, 32)
            wsum[dp, p, yhi, rows] = plus(wsum[dp, p, yhi, rows], yr0[p, i]).astype(BF)
            links.send(("y", off, d, 1), wsum.at[dp, p, yhi], yr1.at[p, i], at.at_y(d))

    def yfinal(off):
        p = at.plane(off)
        for i, d in ((0, 1), (1, -1)):
            links.wait(("y", off, d, 1), yr1.at[p, i], at.at_y(d))
        total = plus(wsum[at.dp, p, at.yhi], yr1[p, 0], yr1[p, 1])
        if off == 0:
            for i, d in ((0, 1), (1, -1)):
                links.wait(("w", d, 3), wzr.at[i, 3], at.at_z(d))
            wg[...] = plus(total, wzr[0, 3], wzr[1, 3])
            return
        if off == 4:
            wy[...] = total.astype(BF)
            for i, d in ((0, 1), (1, -1)):
                rows = pl.ds(i * 32, 32)
                links.send(("w", d, 0), wy.at[rows], wzr.at[i, 0, rows], at.at_z(d))
            return
        d = 1 if off > 0 else -1
        i = half_of(d)
        s = 4 - abs(off)
        if s == 1:
            rows = pl.ds(i * 32, 32)
            rest = pl.ds(32 - i * 32, 32)
            links.wait(("w", d, 0), wzr.at[i, 0, rows], at.at_z(d))
            wzs[i, 0] = total.astype(BF)
            wzs[i, 0, rows] = plus(total[i * 32:i * 32 + 32], wzr[i, 0, rows]).astype(BF)
        else:
            links.wait(("w", d, s - 1), wzr.at[i, s - 1], at.at_z(d))
            wzs[i, s - 1] = plus(total, wzr[i, s - 1]).astype(BF)
        links.send(("w", d, s), wzs.at[i, s - 1], wzr.at[i, s], at.at_z(d))

    def each(step, group):
        for off in GROUPS[group]:
            step(off)

    zsend(0)
    zsend(1, True)
    to_sibling(4)
    xfirst()
    for off in ORDER[1:]:
        to_sibling(off)
    for t in (1, 2, 3):
        links.send(("q", t), dq_h.at[(j + t) % 4], head(dq, 0), at.at_j(t))
    own[0].start()
    each(yfirst, 0)
    each(yfirst, 1)
    each(ysecond, 0)
    zsend(1, False)
    xsecond()
    each(yfirst, 2)
    each(ysecond, 1)
    each(yfinal, 0)
    zsend(2)
    each(yfirst, 3)
    each(ysecond, 2)
    each(yfinal, 1)
    zsend(3)
    xfinal()
    each(yfirst, 4)
    each(ysecond, 3)
    each(yfinal, 2)
    zfinal()
    each(ysecond, 4)
    each(yfinal, 3)
    each(yfinal, 4)
    for t in (1, 2, 3):
        links.wait(("q", t), head(dq, -t), at.at_j(t))
        links.wait(("kv", 0, t), head(dk, -t), at.at_j(t))
        links.wait(("kv", 1, t), head(dv, -t), at.at_j(t))
    for copy in own:
        copy.wait()
    links.drain()
    assert len(links.slots) <= 96, len(links.slots)


def vmem(n):
    return [pl.BlockSpec(memory_space=pltpu.VMEM)] * n


def scatter(dq_h, dkv, px, wgp):
    return pl.pallas_call(
        scatter_kernel,
        out_shape=(
            jax.ShapeDtypeStruct((128, 512), BF),
            jax.ShapeDtypeStruct((128, 512), BF),
            jax.ShapeDtypeStruct((128, 512), BF),
            jax.ShapeDtypeStruct((128, 1024), BF),
            jax.ShapeDtypeStruct((64, 512), F32),
        ),
        in_specs=vmem(4),
        out_specs=tuple(vmem(5)),
        scratch_shapes=[
            pltpu.VMEM((2, 2, 4, 4, 128, HD), BF),
            pltpu.VMEM((2, 2, 3, 4, 128, HD), BF),
            pltpu.VMEM((2, 4, 128, HD), BF),
            pltpu.VMEM((2, 64, 1024), BF),
            pltpu.VMEM((2, 128, 1024), BF),
            pltpu.VMEM((2, 128, 1024), BF),
            pltpu.VMEM((2, 8, 2, 64, 512), BF),
            pltpu.VMEM((2, 8, 2, 64, 512), BF),
            pltpu.VMEM((8, 2, 32, 512), BF),
            pltpu.VMEM((8, 2, 64, 512), BF),
            pltpu.VMEM((64, 512), BF),
            pltpu.VMEM((2, 4, 64, 512), BF),
            pltpu.VMEM((2, 3, 64, 512), BF),
            pltpu.SemaphoreType.DMA((96,)),
            pltpu.SemaphoreType.DMA((96,)),
            pltpu.SemaphoreType.DMA((3,)),
        ],
        compiler_params=pltpu.CompilerParams(
            collective_id=2, has_side_effects=True, vmem_limit_bytes=40 << 20),
        name="scatter",
    )(dq_h, dkv, px, wgp)


def forward_kernel(offsets, posq, qh, kv, wf, ogf, gh, att, lse, scores, top):
    total = dot(ogf[0], wf[pl.ds(0, 1024)])
    for x in (1, 2, 3):
        total += dot(ogf[x], wf[pl.ds(x * 1024, 1024)])
    gh[...] = total.astype(BF)
    q = qh[...]
    row_in = lax.broadcasted_iota(jnp.int32, (128, 512), 0)
    top[...] = jnp.full((8, 512), MASKED, F32)

    @pl.loop(0, 32)
    def _(b):
        rows = pl.ds(pl.multiple_of(b * 128, 128), 128)
        s = dot(kv[0, rows], q, NT) * SCALE2
        s = jnp.where(row_in <= posq[...] - offsets[0, b] * 128, s, MASKED)
        scores[rows] = s
        top[...] = jnp.maximum(top[...], jnp.max(s.reshape(16, 8, 512), axis=0))

    m = jnp.max(top[...], axis=0, keepdims=True)

    def step(b, carry):
        acc, total = carry
        rows = pl.ds(pl.multiple_of(b * 256, 256), 256)
        p = jnp.exp2(scores[rows] - m)
        total = total + jnp.sum(p.reshape(32, 8, 512), axis=0)
        acc = acc + dot(kv[1, rows], p.astype(BF), TN)
        return acc, total

    acc, total = lax.fori_loop(
        0, 16, step, (jnp.zeros((HD, 512), F32), jnp.zeros((8, 512), F32)))
    total = jnp.sum(total, axis=0, keepdims=True)
    att[...] = (acc / total).T.astype(BF)
    lse[...] = m + jnp.log2(total)


def forward(offsets, posq, qh, kv, wf, ogf):
    return pl.pallas_call(
        forward_kernel,
        out_shape=(
            jax.ShapeDtypeStruct((128, 512), BF),
            jax.ShapeDtypeStruct((512, HD), BF),
            jax.ShapeDtypeStruct((1, 512), F32),
        ),
        in_specs=[pl.BlockSpec(memory_space=pltpu.SMEM)] + vmem(5),
        out_specs=tuple(vmem(3)),
        scratch_shapes=[pltpu.VMEM((4096, 512), F32), pltpu.VMEM((8, 512), F32)],
        compiler_params=pltpu.CompilerParams(vmem_limit_bytes=40 << 20),
        name="forward",
    )(offsets, posq, qh, kv, wf, ogf)


def backward_kernel(offsets, posq, qh, kv, wf, ogf, doh, att_tok, att, lse,
                    dq, dkv, px, wgp):
    a = att_tok[...]
    for x in range(4):
        rows = pl.ds(x * 1024, 1024)
        px[x] = dot(a, wf[rows], NT).astype(BF)
        wgp[rows] = dot(ogf[x], a, TN).astype(BF)
    q = qh[...]
    do = doh[...]
    delta = jnp.sum((do.astype(F32) * att[...].astype(F32)).T, axis=0, keepdims=True)
    row_in = lax.broadcasted_iota(jnp.int32, (128, 512), 0)

    def step(b, acc):
        rows = pl.ds(pl.multiple_of(b * 128, 128), 128)
        k, v = kv[0, rows], kv[1, rows]
        s = dot(k, q, NT) * SCALE2
        p = jnp.where(row_in <= posq[...] - offsets[0, b] * 128, jnp.exp2(s - lse[...]), 0.0)
        ds = (p * (dot(v, do, NT) - delta)).astype(BF)
        dkv[1, rows] = dot(p.astype(BF), do).astype(BF)
        dkv[0, rows] = (dot(ds, q) * HD ** -0.5).astype(BF)
        return acc + dot(k, ds, TN)

    acc = lax.fori_loop(0, 32, step, jnp.zeros((HD, 512), F32))
    dq[...] = (acc * HD ** -0.5).T.astype(BF)


def backward(offsets, posq, qh, kv, wf, ogf, doh, att_tok, att, lse):
    return pl.pallas_call(
        backward_kernel,
        out_shape=(
            jax.ShapeDtypeStruct((512, HD), BF),
            jax.ShapeDtypeStruct((2, 4096, HD), BF),
            jax.ShapeDtypeStruct((4, 128, 1024), BF),
            jax.ShapeDtypeStruct((4096, 512), BF),
        ),
        in_specs=[pl.BlockSpec(memory_space=pltpu.SMEM)] + vmem(9),
        out_specs=tuple(vmem(4)),
        compiler_params=pltpu.CompilerParams(vmem_limit_bytes=40 << 20),
        name="backward",
    )(offsets, posq, qh, kv, wf, ogf, doh, att_tok, att, lse)


def on_device(queries, key_rows, value_rows, out_weight, out_grad, block_offsets):
    qh, kv, wf, ogf = gather(queries[0], key_rows[0], value_rows[0], out_weight, out_grad[0])
    plane = lax.axis_index("ctx") // 4
    mine = lax.dynamic_slice(block_offsets, (0, plane * 4), (1, 4))
    posq = (mine.reshape(4, 1) * 128 + jnp.arange(128, dtype=jnp.int32)[None, :]).reshape(1, 512)
    qh = qh.reshape(512, HD)
    kv = kv.reshape(2, 4096, HD)
    wf = wf.reshape(4096, 512)
    gh, att, lse = forward(block_offsets, posq, qh, kv, wf, ogf)
    doh, att_tok = swap(gh, att.reshape(4, 128, HD))
    dq_h, dkv, px, wgp = backward(
        block_offsets, posq, qh, kv, wf, ogf, doh.reshape(512, HD), att_tok, att, lse)
    dq, dk, dv, proj, wg = scatter(
        dq_h.reshape(4, 128, HD), dkv.reshape(2, 8, 4, 128, HD), px,
        wgp.reshape(2, 8, 2, 2, 64, 512))
    return proj[None], dq[None], dk[None], dv[None], wg


def solution(mesh):
    tokens = P("dp", "ctx", "mp")
    features = P(("dp", "ctx"), "mp")
    return jax.shard_map(
        on_device,
        mesh=mesh,
        in_specs=(tokens, tokens, tokens, features, tokens, P("dp", None)),
        out_specs=(tokens, tokens, tokens, tokens, features),
        check_vma=False,
    )
```

```python
import jax
import jax.numpy as jnp
from jax import lax
from jax.experimental import pallas as pl
from jax.experimental.pallas import tpu as pltpu
from jax.sharding import PartitionSpec as P

HD = 128
MASKED = -1e30
MESH = pl.DeviceIdType.MESH
BF = jnp.bfloat16
F32 = jnp.float32
PHASES = ((-1, 1), (-2, 2), (-3, 3), (4,))


class Place:
    def __init__(self):
        self.dp = lax.axis_index("dp")
        self.ctx = lax.axis_index("ctx")
        self.mp = lax.axis_index("mp")
        self.z = self.ctx // 4
        self.j = self.ctx % 4
        self.yhi = self.j // 2
        self.core = self.j % 2
        self.y = self.yhi * 2 + self.dp

    def plane(self, off):
        return (self.z + 8 + off) % 8

    def yblock(self, off):
        y = (self.y + 4 + off) % 4
        return y % 2, y // 2

    def at_z(self, off):
        return {"ctx": self.plane(off) * 4 + self.j}

    def at_y(self, off):
        dp, yhi = self.yblock(off)
        return {"dp": dp, "ctx": self.z * 4 + yhi * 2 + self.core}

    def at_x(self, off):
        return {"mp": (self.mp + 4 + off) % 4}

    def at_j(self, off):
        return {"ctx": self.z * 4 + (self.j + 4 + off) % 4}

    def sibling(self):
        return {"ctx": self.ctx + 1 - 2 * self.core}


def greet(devices):
    barrier = pltpu.get_barrier_semaphore()
    for device in devices:
        pl.semaphore_signal(barrier, inc=1, device_id=device, device_id_type=MESH)
    pl.semaphore_wait(barrier, len(devices))


class Links:
    def __init__(self, send_sems, recv_sems):
        self.send_sems, self.recv_sems = send_sems, recv_sems
        self.slots = {}
        self.sent = []

    def slot(self, name):
        return self.slots.setdefault(name, len(self.slots))

    def copy(self, name, src, dst, device):
        i = self.slot(name)
        return pltpu.make_async_remote_copy(
            src_ref=src, dst_ref=dst, send_sem=self.send_sems.at[i],
            recv_sem=self.recv_sems.at[i], device_id=device, device_id_type=MESH)

    def send(self, name, src, dst, device):
        copy = self.copy(name, src, dst, device)
        copy.start()
        self.sent.append(copy)

    def wait(self, name, dst, device):
        self.copy(name, dst, dst, device).wait_recv()

    def drain(self):
        for copy in self.sent:
            copy.wait_send()


def any_spec(n):
    return [pl.BlockSpec(memory_space=pl.ANY)] * n


GROUPS = ((4,), (3, -3), (2, -2), (1, -1), (0,))
LOG2E = 1.4426950408889634
SCALE = HD ** -0.5
SCALE2 = SCALE * LOG2E
NT = (((1,), (1,)), ((), ()))
TN = (((0,), (0,)), ((), ()))
SIDES = ((0, 1), (1, -1))
SEMS = 176


def dot(a, b, dims=(((1,), (0,)), ((), ()))):
    return lax.dot_general(a, b, dims, preferred_element_type=F32)


def plus(*terms):
    total = terms[0].astype(F32)
    for term in terms[1:]:
        total = total + term.astype(F32)
    return total


def kernel(offsets, q, k, v, w, og, proj, dq, dk, dv, wg,
           qh, kv, wf, ogf, doh, atth, ghs, att_tok, dqh, dkv, px, wgp,
           zr, zs, zfin, xr0, xs, xr1, projs, sibr, wsum, yr0, yr1, wy, wzr, wzs, wgs,
           acc, top, norm, sc, pb, gacc, lse, delta, posq, qacc,
           send_sems, recv_sems, local_sems):
    at = Place()
    z, j, core, mp = at.z, at.j, at.core, at.mp
    greet([at.at_j(1), at.at_j(2), at.at_j(3), at.at_z(1), at.at_z(-1),
           at.at_y(1), at.at_y(-1), at.at_x(1), at.at_x(-1)])
    links = Links(send_sems, recv_sems)

    def head(ref, off):
        return ref.at[:, pl.ds(pl.multiple_of((j + 4 + off) % 4 * HD, HD), HD)]

    def wblock(zoff, yoff, half=None):
        dp, yhi = at.yblock(yoff)
        ref = wf.at[dp, at.plane(zoff), yhi, core]
        return ref if half is None else ref.at[pl.ds(half * 32, 32)]

    own = [
        pltpu.make_async_copy(head(k, 0), kv.at[0, z, j], local_sems.at[0]),
        pltpu.make_async_copy(head(v, 0), kv.at[1, z, j], local_sems.at[1]),
        pltpu.make_async_copy(w, wblock(0, 0), local_sems.at[2]),
        pltpu.make_async_copy(head(q, 0), qh.at[j], local_sems.at[3]),
        pltpu.make_async_copy(og, ogf.at[mp], local_sems.at[4]),
    ]

    def wstep(s):
        for i, d in SIDES:
            off = -d * (1 + s)
            if s < 3:
                links.wait(("wz", d, s), wblock(off, 0), at.at_z(d))
            else:
                links.wait(("wz", d, s), wblock(4, 0, i), at.at_z(d))
            if s < 2:
                links.send(("wz", d, s + 1), wblock(off, 0), wblock(off, 0), at.at_z(d))
            elif s == 2:
                links.send(("wz", d, 3), wblock(off, 0, i), wblock(off, 0, i), at.at_z(d))
        for off in PHASES[s]:
            for d in (1, -1):
                links.send(("wy", off, d), wblock(off, 0), wblock(off, 0), at.at_y(d))

    def forward_y(*offs):
        for off in offs:
            for i, d in SIDES:
                links.wait(("wy", off, d), wblock(off, -d), at.at_y(d))
                links.send(("wyh", off, d), wblock(off, -d, i), wblock(off, -d, i), at.at_y(d))

    def to_sibling(*offs):
        for off in offs:
            for i, d in SIDES:
                links.wait(("wyh", off, d), wblock(off, 2, i), at.at_y(d))
            for dp in (0, 1):
                ref = wf.at[dp, at.plane(off), :, core]
                links.send(("sib", off, dp), ref, ref, at.sibling())

    def ring(a, s):
        for i, d in SIDES:
            if s == 3 and a != i:
                continue
            chunk = kv.at[a, at.plane(-d * (1 + s))]
            links.wait(("z", a, d, s), chunk, at.at_z(d))
            if s < 2 or (s == 2 and a == i):
                links.send(("z", a, d, s + 1), chunk, chunk, at.at_z(d))

    row_in = lax.broadcasted_iota(jnp.int32, (128, 512), 0)

    def allowed(plane, i):
        return row_in <= posq[...] - offsets[0, plane * 4 + i] * 128

    def scores(*offs):
        qs = qh[...].reshape(512, HD)
        best = top[...]
        for n, off in enumerate(offs):
            plane = at.plane(off)

            def tile(i, best):
                s = dot(kv[0, plane, i], qs, NT) * SCALE2
                s = jnp.where(allowed(plane, i), s, MASKED)
                sc[n, i] = s
                return jnp.maximum(best, jnp.max(s.reshape(16, 8, 512), axis=0))

            best = lax.fori_loop(0, 4, tile, best)
        m = jnp.max(best, axis=0, keepdims=True)
        alpha = jnp.exp2(top[0:1] - m)
        top[...] = jnp.broadcast_to(m, (8, 512))
        total = norm[...] * alpha
        for n, off in enumerate(offs):

            def lift(i, total):
                p = jnp.exp2(sc[n, i] - m)
                pb[n, i] = p.astype(BF)
                return total + jnp.sum(p.reshape(16, 8, 512), axis=0)

            total = lax.fori_loop(0, 4, lift, total)
        norm[...] = total
        acc[...] = acc[...] * alpha

    def weigh(*offs):
        for n, off in enumerate(offs):
            values = kv[1, at.plane(off)].reshape(512, HD)
            acc[...] += dot(values, pb[n].reshape(512, 512), TN)

    def og_cols(dp, plane):
        cols = pl.ds(pl.multiple_of(plane % 4 * 256, 256), 256)
        return ogf[dp * 2 + plane // 4, :, cols]

    def head_grad(*offs):
        for off in offs:
            plane = at.plane(off)
            for dp in (0, 1):
                ref = wf.at[dp, plane, :, 1 - core]
                links.wait(("sib", off, dp), ref, at.sibling())
                gacc[...] += dot(og_cols(dp, plane), wf[dp, plane].reshape(256, 512))

    for copy in own:
        copy.start()
    for a, ref in ((0, k), (1, v)):
        for t in (1, 2, 3):
            links.send(("kv", a, t), head(ref, t), kv.at[a, z, j], at.at_j(t))
    for d in (1, -1):
        links.send(("wz", d, 0), w, wblock(0, 0), at.at_z(d))
        links.send(("wy", 0, d), w, wblock(0, 0), at.at_y(d))
    for t in (1, 2, 3):
        links.send(("q", t), head(q, t), qh.at[j], at.at_j(t))
    for d in (1, -1):
        links.send(("og", d, 0), og, ogf.at[mp], at.at_x(d))
    lane = lax.broadcasted_iota(jnp.int32, (1, 512), 1)
    place = lane % 128
    for i in range(4):
        place = place + jnp.where(lane // 128 == i, offsets[0, z * 4 + i] * 128, 0)
    posq[...] = place
    acc[...] = jnp.zeros_like(acc)
    gacc[...] = jnp.zeros_like(gacc)
    qacc[...] = jnp.zeros_like(qacc)
    norm[...] = jnp.zeros_like(norm)
    top[...] = jnp.full_like(top, MASKED)

    for a in (0, 1):
        own[a].wait()
        for t in (1, 2, 3):
            links.wait(("kv", a, t), kv.at[a, z, (j + 4 - t) % 4], at.at_j(t))
        for d in (1, -1):
            links.send(("z", a, d, 0), kv.at[a, z], kv.at[a, z], at.at_z(d))
    own[2].wait()
    wstep(0)
    own[3].wait()
    for t in (1, 2, 3):
        links.wait(("q", t), qh.at[(j + 4 - t) % 4], at.at_j(t))
    scores(0)
    weigh(0)
    wstep(1)
    forward_y(0)
    ring(0, 0)
    scores(-1, 1)
    own[4].wait()
    for i, d in SIDES:
        links.wait(("og", d, 0), ogf.at[(mp + 4 - d) % 4], at.at_x(d))
        half = ogf.at[(mp + 4 - d) % 4, pl.ds(i * 64, 64)]
        links.send(("og", d, 1), half, half, at.at_x(d))
    ring(1, 0)
    wstep(2)
    forward_y(-1, 1)
    weigh(-1, 1)
    to_sibling(0)
    ring(0, 1)
    scores(-2, 2)
    wstep(3)
    ring(1, 1)
    forward_y(-2, 2)
    weigh(-2, 2)
    to_sibling(-1, 1)
    for i, d in SIDES:
        half = ogf.at[(mp + 2) % 4, pl.ds(i * 64, 64)]
        links.wait(("og", d, 1), half, at.at_x(d))
    head_grad(0)
    ring(0, 2)
    scores(-3, 3)
    forward_y(-3, 3)
    to_sibling(-2, 2)
    ring(1, 2)
    weigh(-3, 3)
    forward_y(4)
    to_sibling(-3, 3)
    head_grad(-1, 1, -2, 2)
    to_sibling(4)
    ring(0, 3)
    scores(4)
    head_grad(-3, 3, 4)
    ghs[...] = gacc[...].astype(BF)
    for t in (1, 2, 3):
        links.send(("g", t), head(ghs, t), doh.at[j], at.at_j(t))
    own.append(pltpu.make_async_copy(head(ghs, 0), doh.at[j], local_sems.at[5]))
    own[5].start()
    ring(1, 3)
    weigh(4)
    total = jnp.sum(norm[...], axis=0, keepdims=True)
    atth[...] = (acc[...] / total).T.astype(BF).reshape(4, 128, HD)
    lse[...] = top[0:1] + jnp.log2(total)
    for t in (1, 2, 3):
        links.send(("a", t), atth.at[(j + t) % 4], head(att_tok, 0), at.at_j(t))
    own.append(pltpu.make_async_copy(atth.at[j], head(att_tok, 0), local_sems.at[6]))
    own[6].start()

    def backward(off):
        plane = at.plane(off)
        qs = qh[...].reshape(512, HD)
        do = doh[...].reshape(512, HD)

        def tile(i, carry):
            kt, vt = kv[0, plane, i], kv[1, plane, i]
            s = dot(kt, qs, NT) * SCALE2
            p = jnp.where(allowed(plane, i), jnp.exp2(s - lse[...]), 0.0)
            ds = (p * (dot(vt, do, NT) - delta[...])).astype(BF)
            dkv[1, plane, i] = dot(p.astype(BF), do).astype(BF)
            dkv[0, plane, i] = (dot(ds, qs) * SCALE).astype(BF)
            qacc[...] += dot(kt, ds, TN)
            return carry

        lax.fori_loop(0, 4, tile, 0)

    def zsend(s, raw=None):
        for i, d in SIDES:
            for a in (0, 1):
                if s == 0 and a != i:
                    continue
                if raw is not None and raw != (a != i):
                    continue
                p = at.plane(d * (4 - s))
                if s == 0 or (s == 1 and a != i):
                    src = dkv.at[a, p]
                else:
                    links.wait(("rz", a, d, s - 1), zr.at[a, i, s - 1], at.at_z(d))
                    zs[a, i, s - 1] = plus(dkv[a, p], zr[a, i, s - 1]).astype(BF)
                    src = zs.at[a, i, s - 1]
                links.send(("rz", a, d, s), src, zr.at[a, i, s], at.at_z(d))

    def zfinal():
        for a, out in ((0, dk), (1, dv)):
            for i, d in SIDES:
                links.wait(("rz", a, d, 3), zr.at[a, i, 3], at.at_z(d))
            zfin[a] = plus(dkv[a, z], zr[a, 0, 3], zr[a, 1, 3]).astype(BF)
            for t in (1, 2, 3):
                links.send(("dkv", a, t), zfin.at[a, (j + t) % 4], head(out, 0), at.at_j(t))
            copy = pltpu.make_async_copy(zfin.at[a, j], head(out, 0), local_sems.at[7 + a])
            copy.start()
            own.append(copy)

    def project(off):
        x = (mp + 4 + off) % 4
        rows = wf[x // 2, pl.ds(pl.multiple_of(x % 2 * 4, 4), 4)].reshape(1024, 512)
        px[x] = dot(att_tok[...], rows, NT).astype(BF)

    def xfirst():
        for i, d in SIDES:
            links.send(("x", d, 0), px.at[(mp + 2) % 4, pl.ds(i * 64, 64)], xr0.at[i], at.at_x(d))

    def xsecond():
        for i, d in SIDES:
            chunk = (mp + 4 + d) % 4
            links.wait(("x", d, 0), xr0.at[i], at.at_x(d))
            xs[i, pl.ds(i * 64, 64)] = plus(px[chunk, pl.ds(i * 64, 64)], xr0[i]).astype(BF)
            xs[i, pl.ds(64 - i * 64, 64)] = px[chunk, pl.ds(64 - i * 64, 64)]
            links.send(("x", d, 1), xs.at[i], xr1.at[i], at.at_x(d))

    def xfinal():
        for i, d in SIDES:
            links.wait(("x", d, 1), xr1.at[i], at.at_x(d))
        projs[...] = plus(px[mp], xr1[0], xr1[1]).astype(BF)
        copy = pltpu.make_async_copy(projs, proj, local_sems.at[9])
        copy.start()
        own.append(copy)

    def weight_grad(*offs):
        for off in offs:
            p = at.plane(off)
            for dp in (0, 1):
                part = dot(og_cols(dp, p), att_tok[...], TN).astype(BF)
                wgp[dp, p] = part.reshape(2, 2, 64, 512)
                links.send(("wsib", off, dp), wgp.at[dp, p, :, 1 - core], sibr.at[dp, p], at.sibling())

    def yfirst(off):
        p = at.plane(off)
        for dp in (0, 1):
            links.wait(("wsib", off, dp), sibr.at[dp, p], at.sibling())
        for dp in (0, 1):
            for yhi in (0, 1):
                wsum[dp, p, yhi] = plus(wgp[dp, p, yhi, core], sibr[dp, p, yhi]).astype(BF)
        dp, yhi = at.yblock(2)
        for i, d in SIDES:
            links.send(("y", off, d, 0), wsum.at[dp, p, yhi, pl.ds(i * 32, 32)], yr0.at[p, i], at.at_y(d))

    def ysecond(off):
        p = at.plane(off)
        for i, d in SIDES:
            dp, yhi = at.yblock(d)
            links.wait(("y", off, d, 0), yr0.at[p, i], at.at_y(d))
            rows = pl.ds(i * 32, 32)
            wsum[dp, p, yhi, rows] = plus(wsum[dp, p, yhi, rows], yr0[p, i]).astype(BF)
            links.send(("y", off, d, 1), wsum.at[dp, p, yhi], yr1.at[p, i], at.at_y(d))

    def yfinal(off):
        p = at.plane(off)
        for i, d in SIDES:
            links.wait(("y", off, d, 1), yr1.at[p, i], at.at_y(d))
        total = plus(wsum[at.dp, p, at.yhi], yr1[p, 0], yr1[p, 1])
        if off == 0:
            for i, d in SIDES:
                links.wait(("w", d, 3), wzr.at[i, 3], at.at_z(d))
            wgs[...] = plus(total, wzr[0, 3], wzr[1, 3])
            copy = pltpu.make_async_copy(wgs, wg, local_sems.at[10])
            copy.start()
            own.append(copy)
            return
        if off == 4:
            wy[...] = total.astype(BF)
            for i, d in SIDES:
                rows = pl.ds(i * 32, 32)
                links.send(("w", d, 0), wy.at[rows], wzr.at[i, 0, rows], at.at_z(d))
            return
        d = 1 if off > 0 else -1
        i = (1 - d) // 2
        s = 4 - abs(off)
        if s == 1:
            rows = pl.ds(i * 32, 32)
            links.wait(("w", d, 0), wzr.at[i, 0, rows], at.at_z(d))
            wzs[i, 0] = total.astype(BF)
            wzs[i, 0, rows] = plus(total[i * 32:i * 32 + 32], wzr[i, 0, rows]).astype(BF)
        else:
            links.wait(("w", d, s - 1), wzr.at[i, s - 1], at.at_z(d))
            wzs[i, s - 1] = plus(total, wzr[i, s - 1]).astype(BF)
        links.send(("w", d, s), wzs.at[i, s - 1], wzr.at[i, s], at.at_z(d))

    def each(step, group):
        for off in GROUPS[group]:
            step(off)

    own[5].wait()
    for t in (1, 2, 3):
        links.wait(("g", t), doh.at[(j + 4 - t) % 4], at.at_j(t))
    products = (doh[...].astype(F32) * atth[...].astype(F32)).reshape(512, HD)
    delta[...] = jnp.sum(products.T, axis=0, keepdims=True)
    backward(4)
    zsend(0)
    own[6].wait()
    for t in (1, 2, 3):
        links.wait(("a", t), head(att_tok, -t), at.at_j(t))
    weight_grad(4, 3, -3)
    project(2)
    xfirst()
    backward(3)
    backward(-3)
    zsend(1, True)
    weight_grad(2, -2, 1, -1, 0)
    each(yfirst, 0)
    project(1)
    project(-1)
    zsend(1, False)
    each(yfirst, 1)
    xsecond()
    backward(2)
    each(ysecond, 0)
    backward(-2)
    each(yfirst, 2)
    each(ysecond, 1)
    zsend(2)
    each(yfinal, 0)
    backward(1)
    each(yfirst, 3)
    backward(-1)
    each(ysecond, 2)
    each(yfinal, 1)
    zsend(3)
    project(0)
    xfinal()
    each(yfirst, 4)
    backward(0)
    each(ysecond, 3)
    each(yfinal, 2)
    dqh[...] = (qacc[...] * SCALE).T.astype(BF).reshape(4, 128, HD)
    for t in (1, 2, 3):
        links.send(("dq", t), dqh.at[(j + t) % 4], head(dq, 0), at.at_j(t))
    copy = pltpu.make_async_copy(dqh.at[j], head(dq, 0), local_sems.at[11])
    copy.start()
    own.append(copy)
    each(ysecond, 4)
    zfinal()
    each(yfinal, 3)
    each(yfinal, 4)
    for t in (1, 2, 3):
        links.wait(("dq", t), head(dq, -t), at.at_j(t))
        links.wait(("dkv", 0, t), head(dk, -t), at.at_j(t))
        links.wait(("dkv", 1, t), head(dv, -t), at.at_j(t))
    for copy in own[7:]:
        copy.wait()
    links.drain()
    assert len(links.slots) <= SEMS, len(links.slots)


def on_device(queries, key_rows, value_rows, out_weight, out_grad, block_offsets):
    heads = jax.ShapeDtypeStruct((128, 512), BF)
    proj, dq, dk, dv, wg = pl.pallas_call(
        kernel,
        out_shape=(
            jax.ShapeDtypeStruct((128, 1024), BF), heads, heads, heads,
            jax.ShapeDtypeStruct((64, 512), F32),
        ),
        in_specs=[pl.BlockSpec(memory_space=pltpu.SMEM)] + any_spec(5),
        out_specs=tuple(any_spec(5)),
        scratch_shapes=[
            pltpu.VMEM((4, 128, HD), BF),
            pltpu.VMEM((2, 8, 4, 128, HD), BF),
            pltpu.VMEM((2, 8, 2, 2, 64, 512), BF),
            pltpu.VMEM((4, 128, 1024), BF),
            pltpu.VMEM((4, 128, HD), BF),
            pltpu.VMEM((4, 128, HD), BF),
            pltpu.VMEM((128, 512), BF),
            pltpu.VMEM((128, 512), BF),
            pltpu.VMEM((4, 128, HD), BF),
            pltpu.VMEM((2, 8, 4, 128, HD), BF),
            pltpu.VMEM((4, 128, 1024), BF),
            pltpu.VMEM((2, 8, 2, 2, 64, 512), BF),
            pltpu.VMEM((2, 2, 4, 4, 128, HD), BF),
            pltpu.VMEM((2, 2, 3, 4, 128, HD), BF),
            pltpu.VMEM((2, 4, 128, HD), BF),
            pltpu.VMEM((2, 64, 1024), BF),
            pltpu.VMEM((2, 128, 1024), BF),
            pltpu.VMEM((2, 128, 1024), BF),
            pltpu.VMEM((128, 1024), BF),
            pltpu.VMEM((2, 8, 2, 64, 512), BF),
            pltpu.VMEM((2, 8, 2, 64, 512), BF),
            pltpu.VMEM((8, 2, 32, 512), BF),
            pltpu.VMEM((8, 2, 64, 512), BF),
            pltpu.VMEM((64, 512), BF),
            pltpu.VMEM((2, 4, 64, 512), BF),
            pltpu.VMEM((2, 3, 64, 512), BF),
            pltpu.VMEM((64, 512), F32),
            pltpu.VMEM((HD, 512), F32),
            pltpu.VMEM((8, 512), F32),
            pltpu.VMEM((8, 512), F32),
            pltpu.VMEM((2, 4, 128, 512), F32),
            pltpu.VMEM((2, 4, 128, 512), BF),
            pltpu.VMEM((128, 512), F32),
            pltpu.VMEM((1, 512), F32),
            pltpu.VMEM((1, 512), F32),
            pltpu.VMEM((1, 512), jnp.int32),
            pltpu.VMEM((HD, 512), F32),
            pltpu.SemaphoreType.DMA((SEMS,)),
            pltpu.SemaphoreType.DMA((SEMS,)),
            pltpu.SemaphoreType.DMA((12,)),
        ],
        compiler_params=pltpu.CompilerParams(
            collective_id=0, has_side_effects=True, vmem_limit_bytes=62 << 20),
        name="whole",
    )(block_offsets, queries[0], key_rows[0], value_rows[0], out_weight, out_grad[0])
    return proj[None], dq[None], dk[None], dv[None], wg


def solution(mesh):
    tokens = P("dp", "ctx", "mp")
    features = P(("dp", "ctx"), "mp")
    return jax.shard_map(
        on_device,
        mesh=mesh,
        in_specs=(tokens, tokens, tokens, features, tokens, P("dp", None)),
        out_specs=(tokens, tokens, tokens, tokens, features),
        check_vma=False,
    )
```

```python
import jax
import jax.numpy as jnp
from jax import lax
from jax.experimental import pallas as pl
from jax.experimental.pallas import tpu as pltpu
from jax.sharding import PartitionSpec as P

HD = 128
MASKED = -1e30
MESH = pl.DeviceIdType.MESH
BF = jnp.bfloat16
F32 = jnp.float32
PHASES = ((-1, 1), (-2, 2), (-3, 3), (4,))


class Place:
    def __init__(self):
        self.dp = lax.axis_index("dp")
        self.ctx = lax.axis_index("ctx")
        self.mp = lax.axis_index("mp")
        self.z = self.ctx // 4
        self.j = self.ctx % 4
        self.yhi = self.j // 2
        self.core = self.j % 2
        self.y = self.yhi * 2 + self.dp

    def plane(self, off):
        return (self.z + 8 + off) % 8

    def yblock(self, off):
        y = (self.y + 4 + off) % 4
        return y % 2, y // 2

    def at_z(self, off):
        return {"ctx": self.plane(off) * 4 + self.j}

    def at_y(self, off):
        dp, yhi = self.yblock(off)
        return {"dp": dp, "ctx": self.z * 4 + yhi * 2 + self.core}

    def at_x(self, off):
        return {"mp": (self.mp + 4 + off) % 4}

    def at_j(self, off):
        return {"ctx": self.z * 4 + (self.j + 4 + off) % 4}

    def sibling(self):
        return {"ctx": self.ctx + 1 - 2 * self.core}


def greet(devices):
    barrier = pltpu.get_barrier_semaphore()
    for device in devices:
        pl.semaphore_signal(barrier, inc=1, device_id=device, device_id_type=MESH)
    pl.semaphore_wait(barrier, len(devices))


class Links:
    def __init__(self, send_sems, recv_sems):
        self.send_sems, self.recv_sems = send_sems, recv_sems
        self.slots = {}
        self.leaving = [None] * SENDS
        self.count = 0

    def copy(self, name, src, dst, device, sender):
        i = self.slots.setdefault(name, len(self.slots))
        return pltpu.make_async_remote_copy(
            src_ref=src, dst_ref=dst, send_sem=self.send_sems.at[sender],
            recv_sem=self.recv_sems.at[i], device_id=device, device_id_type=MESH)

    def send(self, name, src, dst, device):
        i = self.count % SENDS
        self.count += 1
        if self.leaving[i] is not None:
            self.leaving[i].wait_send()
        self.leaving[i] = self.copy(name, src, dst, device, i)
        self.leaving[i].start()

    def wait(self, name, dst, device):
        self.copy(name, dst, dst, device, 0).wait_recv()

    def drain(self):
        for copy in self.leaving:
            copy.wait_send()


def vmem(n):
    return [pl.BlockSpec(memory_space=pltpu.VMEM)] * n


def any_spec(n):
    return [pl.BlockSpec(memory_space=pl.ANY)] * n


GROUPS = ((4,), (3, -3), (2, -2), (1, -1), (0,))
LOG2E = 1.4426950408889634
SCALE = HD ** -0.5
SCALE2 = SCALE * LOG2E
NT = (((1,), (1,)), ((), ()))
TN = (((0,), (0,)), ((), ()))
SIDES = ((0, 1), (1, -1))
SENDS = 32
RECEIVES = 131
ORDER = (
    ("K0",), ("W0",), ("WY0",), ("Q0",), ("W", 0, -1),
    ("W", 0, 1), ("OG0",), ("V0",), ("WY", 1), ("WY", -1),
    ("RA", 0), ("W", 1, 1), ("FY", 0, 1), ("FY", 0, -1), ("W", 1, -1),
    ("WY", 2), ("WY", -2), ("RA", 1), ("W", 2, -1), ("W", 2, 1),
    ("R", 0, 0, -1), ("WY", -3), ("SC", 0), ("R", 0, 0, 1), ("FY", 1, -1),
    ("FY", -2, 1), ("WY", 3), ("OG", 1), ("R", 1, 0, 1), ("W", 3, -1),
    ("FY", 2, 1), ("FY", -1, -1), ("FY", -1, 1), ("R", 1, 0, -1), ("W", 3, 1),
    ("OG", -1), ("WE", 0), ("FY", -2, -1), ("FY", 1, 1), ("SC", 1),
    ("FY", -3, -1), ("R", 0, 1, -1), ("WY", 4), ("S", 0), ("R", 0, 1, 1),
    ("FY", 2, -1), ("FY", -3, 1), ("WE", 1), ("S", -1), ("FY", 3, -1),
    ("FY", 3, 1), ("R", 1, 1, 1), ("FY", 4, -1), ("S", -2), ("R", 1, 1, -1),
    ("FY", 4, 1), ("S", 2), ("SC", 2), ("OL",), ("HG", -2),
    ("S", -3), ("S", 3), ("S", 1), ("HG", 2), ("R", 0, 2, 1),
    ("HG", 0), ("S", 4), ("HG", -1), ("R", 0, 2, -1), ("HG", -3),
    ("R", 1, 2, -1), ("WE", 2), ("HG", 1), ("HG", 4), ("HG", 3),
    ("GH",), ("R", 1, 2, 1), ("SC", 3), ("R", 0, 3, 1), ("WE", 3),
    ("SC", 4), ("R", 1, 3, -1), ("WE", 4), ("FIN",), ("DEL",),
    ("B", 4), ("Z", 1, 0, -1), ("Z", 0, 0, 1), ("B", 3), ("B", -3),
    ("Z", 0, 1, -1), ("Z", 1, 1, 1), ("B", 2), ("ATT",), ("WG", 4),
    ("WG", 3), ("WG", -3), ("WG", 2), ("B", -2), ("Y1", 4),
    ("Z", 1, 1, -1), ("Z", 0, 1, 1), ("WG", -2), ("Y1", -3), ("Y1", 3),
    ("WG", -1), ("Y1", 2), ("WG", 1), ("Z", 0, 2, -1), ("Y1", -2),
    ("Z", 1, 2, 1), ("Y2", 4, 1), ("WG", 0), ("Y2", 4, -1), ("PX", 2),
    ("Y2", -3, 1), ("Y1", -1), ("Y2", -3, -1), ("Y1", 1), ("Z", 1, 2, -1),
    ("Z", 0, 2, 1), ("Y2", 3, -1), ("PX", 1), ("B", -1), ("XF",),
    ("Y2", 3, 1), ("B", 1), ("Y3", 4), ("Z", 0, 3, -1), ("Y2", -2, 1),
    ("Z", 1, 3, 1), ("Y2", 2, 1), ("Y1", 0), ("Y2", -2, -1), ("B", 0),
    ("Y2", 1, 1), ("Y2", 2, -1), ("DQ",), ("Y2", -1, 1), ("Y3", -3),
    ("Y3", 3), ("PX", -1), ("Y2", 1, -1), ("Z", 1, 3, -1), ("XS", -1),
    ("Z", 0, 3, 1), ("XS", 1), ("Y2", -1, -1), ("Y2", 0, -1), ("Y2", 0, 1),
    ("Y3", 2), ("Y3", -2), ("ZF", 1), ("PX", 0), ("ZF", 0),
    ("Y3", -1), ("Y3", 1), ("XE",), ("Y3", 0), ("END",),
)


def dot(a, b, dims=(((1,), (0,)), ((), ()))):
    return lax.dot_general(a, b, dims, preferred_element_type=F32)


def plus(*terms):
    total = terms[0].astype(F32)
    for term in terms[1:]:
        total = total + term.astype(F32)
    return total


def kernel(offsets, q, k, v, w, og, proj, dq, dk, dv, wg,
           qh, kv, wf, ogf, doh, atth, ghs, att_tok, dqh, dkv, px, wgp,
           zr, zs, zfin, xr0, xs, xr1, projs, sibr, wsum, yr0, yr1, wyb, wzr, wzs, wgs,
           acc, top, norm, sc, pb, gacc, lse, delta, posq, qacc,
           send_sems, recv_sems, local_sems):
    at = Place()
    z, j, core, mp = at.z, at.j, at.core, at.mp
    greet([at.at_j(1), at.at_j(2), at.at_j(3), at.at_z(1), at.at_z(-1),
           at.at_y(1), at.at_y(-1), at.at_x(1), at.at_x(-1)])
    links = Links(send_sems, recv_sems)

    def head(ref, off):
        return ref.at[:, pl.ds(pl.multiple_of((j + 4 + off) % 4 * HD, HD), HD)]

    def wblock(zoff, yoff, half=None):
        dp, yhi = at.yblock(yoff)
        ref = wf.at[dp, at.plane(zoff), yhi, core]
        return ref if half is None else ref.at[pl.ds(half * 32, 32)]

    own = {}

    def keep(name, src, dst):
        own[name] = pltpu.make_async_copy(src, dst, local_sems.at[len(own)])
        own[name].start()

    def scatter_heads(name, blocks, dst):
        for t in (1, 2, 3):
            links.send(name, blocks(t), dst, at.at_j(t))
        keep(name, blocks(0), dst)

    def await_heads(name, three):
        links.wait(name, three, at.at_j(1))
        own[name].wait()

    three_blocks = pl.ds(0, 3)
    three_heads = pl.ds(0, 3 * HD)

    def k0():
        scatter_heads("k", lambda t: head(k, t), kv.at[0, z, j])

    def v0():
        scatter_heads("v", lambda t: head(v, t), kv.at[1, z, j])

    def q0():
        scatter_heads("q", lambda t: head(q, t), qh.at[j])

    def w0():
        keep("w", w, wblock(0, 0))
        for d in (1, -1):
            links.send(("wz", d, 0), w, wblock(0, 0), at.at_z(d))

    def wy0():
        for d in (1, -1):
            links.send(("wy", 0, d), w, wblock(0, 0), at.at_y(d))

    def og0():
        for d in (1, -1):
            links.send(("og", d, 0), og, ogf.at[mp], at.at_x(d))
        keep("og", og, ogf.at[mp])

    def ring_start(a):
        await_heads("kv"[a], kv.at[a, z, three_blocks])
        for d in (1, -1):
            links.send(("z", a, d, 0), kv.at[a, z], kv.at[a, z], at.at_z(d))

    def ring(a, s, d):
        i = (1 - d) // 2
        chunk = kv.at[a, at.plane(-d * (1 + s))]
        links.wait(("z", a, d, s), chunk, at.at_z(d))
        if s < 2 or (s == 2 and a == i):
            links.send(("z", a, d, s + 1), chunk, chunk, at.at_z(d))

    def wstep(s, d):
        i = (1 - d) // 2
        block = wblock(-d * (1 + s), 0) if s < 3 else wblock(4, 0, i)
        links.wait(("wz", d, s), block, at.at_z(d))
        if s < 2:
            links.send(("wz", d, s + 1), block, block, at.at_z(d))
        elif s == 2:
            half = wblock(-d * 3, 0, i)
            links.send(("wz", d, 3), half, half, at.at_z(d))

    def wy(off):
        for d in (1, -1):
            links.send(("wy", off, d), wblock(off, 0), wblock(off, 0), at.at_y(d))

    def wforward(off, d):
        i = (1 - d) // 2
        links.wait(("wy", off, d), wblock(off, -d), at.at_y(d))
        links.send(("wyh", off), wblock(off, -d, i), wblock(off, -d, i), at.at_y(d))

    def wshare(off):
        if off == 0:
            own["w"].wait()
        links.wait(("wyh", off), wblock(off, 2), at.at_y(1))
        for dp in (0, 1):
            ref = wf.at[dp, at.plane(off), :, core]
            links.send(("sib", off), ref, ref, at.sibling())

    def ogstep(d):
        slot = ogf.at[(mp + 4 - d) % 4]
        links.wait(("og", d, 0), slot, at.at_x(d))
        half = slot.at[pl.ds((1 - d) // 2 * 64, 64)]
        links.send("ogh", half, half, at.at_x(d))

    def oglast():
        own["og"].wait()
        links.wait("ogh", ogf.at[(mp + 2) % 4], at.at_x(1))

    row_in = lax.broadcasted_iota(jnp.int32, (128, 512), 0)

    def allowed(plane):
        return jnp.concatenate(
            [row_in <= posq[...] - offsets[0, plane * 4 + i] * 128 for i in range(4)], axis=0)

    def fold(op, rows):
        return op(rows.reshape(64, 8, 512), axis=0)

    def begin():
        lane = lax.broadcasted_iota(jnp.int32, (1, 512), 1)
        place = lane % 128
        for i in range(4):
            place = place + jnp.where(lane // 128 == i, offsets[0, z * 4 + i] * 128, 0)
        posq[...] = place
        acc[...] = jnp.zeros_like(acc)
        gacc[...] = jnp.zeros_like(gacc)
        qacc[...] = jnp.zeros_like(qacc)
        norm[...] = jnp.zeros_like(norm)
        top[...] = jnp.full_like(top, MASKED)

    def planes(n):
        return (n,) if n in (0, 4) else (-n, n)

    def scores(n):
        if n == 0:
            begin()
            await_heads("q", qh.at[three_blocks])
        qs = qh[...].reshape(512, HD)
        best = top[...]
        for i, off in enumerate(planes(n)):
            plane = at.plane(off)
            s = dot(kv[0, plane].reshape(512, HD), qs, NT) * SCALE2
            s = jnp.where(allowed(plane), s, MASKED)
            sc[i] = s
            best = jnp.maximum(best, fold(jnp.max, s))
        m = jnp.max(best, axis=0, keepdims=True)
        alpha = jnp.exp2(top[0:1] - m)
        top[...] = jnp.broadcast_to(m, (8, 512))
        total = norm[...] * alpha
        for i, off in enumerate(planes(n)):
            p = jnp.exp2(sc[i] - m)
            pb[i] = p.astype(BF)
            total = total + fold(jnp.sum, p)
        norm[...] = total
        acc[...] = acc[...] * alpha

    def weigh(n):
        for i, off in enumerate(planes(n)):
            acc[...] += dot(kv[1, at.plane(off)].reshape(512, HD), pb[i], TN)

    def og_cols(dp, plane):
        cols = pl.ds(pl.multiple_of(plane % 4 * 256, 256), 256)
        return ogf[dp * 2 + plane // 4, :, cols]

    def head_grad(off):
        plane = at.plane(off)
        links.wait(("sib", off), wf.at[:, plane, :, 1 - core], at.sibling())
        gacc[...] += sum(
            dot(og_cols(dp, plane), wf[dp, plane].reshape(256, 512)) for dp in (0, 1))

    def send_grad():
        ghs[...] = gacc[...].astype(BF)
        scatter_heads("g", lambda t: head(ghs, t), doh.at[j])

    def finish_attention():
        total = jnp.sum(norm[...], axis=0, keepdims=True)
        atth[...] = (acc[...] / total).T.astype(BF).reshape(4, 128, HD)
        lse[...] = top[0:1] + jnp.log2(total)
        scatter_heads("a", lambda t: atth.at[(j + t) % 4], head(att_tok, 0))

    def deltas():
        await_heads("g", doh.at[three_blocks])
        products = (doh[...].astype(F32) * atth[...].astype(F32)).reshape(512, HD)
        delta[...] = jnp.sum(products.T, axis=0, keepdims=True)

    def backward(off):
        plane = at.plane(off)
        qs = qh[...].reshape(512, HD)
        do = doh[...].reshape(512, HD)
        ks, vs = kv[0, plane].reshape(512, HD), kv[1, plane].reshape(512, HD)
        s = dot(ks, qs, NT) * SCALE2
        p = jnp.where(allowed(plane), jnp.exp2(s - lse[...]), 0.0)
        ds = (p * (dot(vs, do, NT) - delta[...])).astype(BF)
        dkv[1, plane] = dot(p.astype(BF), do).astype(BF).reshape(4, 128, HD)
        dkv[0, plane] = (dot(ds, qs) * SCALE).astype(BF).reshape(4, 128, HD)
        qacc[...] += dot(ks, ds, TN)

    def zsend(a, s, d):
        i = (1 - d) // 2
        p = at.plane(d * (4 - s))
        if s == 0 or (s == 1 and a != i):
            src = dkv.at[a, p]
        else:
            links.wait(("rz", a, d, s - 1), zr.at[a, i, s - 1], at.at_z(d))
            zs[a, i, s - 1] = plus(dkv[a, p], zr[a, i, s - 1]).astype(BF)
            src = zs.at[a, i, s - 1]
        links.send(("rz", a, d, s), src, zr.at[a, i, s], at.at_z(d))

    def zfinal(a):
        for i, d in SIDES:
            links.wait(("rz", a, d, 3), zr.at[a, i, 3], at.at_z(d))
        zfin[a] = plus(dkv[a, z], zr[a, 0, 3], zr[a, 1, 3]).astype(BF)
        scatter_heads(("dk", "dv")[a], lambda t: zfin.at[a, (j + t) % 4], head((dk, dv)[a], 0))

    def project(off):
        x = (mp + 4 + off) % 4
        rows = wf[x // 2, pl.ds(pl.multiple_of(x % 2 * 4, 4), 4)].reshape(1024, 512)
        px[x] = dot(att_tok[...], rows, NT).astype(BF)

    def xfirst():
        for i, d in SIDES:
            links.send(("x", d, 0), px.at[(mp + 2) % 4, pl.ds(i * 64, 64)], xr0.at[i], at.at_x(d))

    def xsecond(d):
        i = (1 - d) // 2
        chunk = (mp + 4 + d) % 4
        links.wait(("x", d, 0), xr0.at[i], at.at_x(d))
        xs[i, pl.ds(i * 64, 64)] = plus(px[chunk, pl.ds(i * 64, 64)], xr0[i]).astype(BF)
        xs[i, pl.ds(64 - i * 64, 64)] = px[chunk, pl.ds(64 - i * 64, 64)]
        links.send(("x", d, 1), xs.at[i], xr1.at[i], at.at_x(d))

    def xfinal():
        for i, d in SIDES:
            links.wait(("x", d, 1), xr1.at[i], at.at_x(d))
        projs[...] = plus(px[mp], xr1[0], xr1[1]).astype(BF)
        keep("proj", projs, proj)

    def await_attended():
        await_heads("a", att_tok.at[:, three_heads])

    def weight_grad(off):
        p = at.plane(off)
        for dp in (0, 1):
            part = dot(og_cols(dp, p), att_tok[...], TN).astype(BF)
            wgp[dp, p] = part.reshape(2, 2, 64, 512)
            links.send(("wsib", off), wgp.at[dp, p, :, 1 - core], sibr.at[dp, p], at.sibling())

    def yfirst(off):
        p = at.plane(off)
        links.wait(("wsib", off), sibr.at[:, p], at.sibling())
        for dp in (0, 1):
            for yhi in (0, 1):
                wsum[dp, p, yhi] = plus(wgp[dp, p, yhi, core], sibr[dp, p, yhi]).astype(BF)
        dp, yhi = at.yblock(2)
        for i, d in SIDES:
            links.send(("y", off, d, 0), wsum.at[dp, p, yhi, pl.ds(i * 32, 32)], yr0.at[p, i], at.at_y(d))

    def ysecond(off, d):
        p = at.plane(off)
        i = (1 - d) // 2
        dp, yhi = at.yblock(d)
        links.wait(("y", off, d, 0), yr0.at[p, i], at.at_y(d))
        rows = pl.ds(i * 32, 32)
        wsum[dp, p, yhi, rows] = plus(wsum[dp, p, yhi, rows], yr0[p, i]).astype(BF)
        links.send(("y", off, d, 1), wsum.at[dp, p, yhi], yr1.at[p, i], at.at_y(d))

    def yfinal(off):
        p = at.plane(off)
        for i, d in SIDES:
            links.wait(("y", off, d, 1), yr1.at[p, i], at.at_y(d))
        total = plus(wsum[at.dp, p, at.yhi], yr1[p, 0], yr1[p, 1])
        if off == 0:
            for i, d in SIDES:
                links.wait(("w", d, 3), wzr.at[i, 3], at.at_z(d))
            wgs[...] = plus(total, wzr[0, 3], wzr[1, 3])
            keep("wg", wgs, wg)
            return
        if off == 4:
            wyb[...] = total.astype(BF)
            for i, d in SIDES:
                rows = pl.ds(i * 32, 32)
                links.send(("w", d, 0), wyb.at[rows], wzr.at[i, 0, rows], at.at_z(d))
            return
        d = 1 if off > 0 else -1
        i = (1 - d) // 2
        s = 4 - abs(off)
        if s == 1:
            rows = pl.ds(i * 32, 32)
            links.wait(("w", d, 0), wzr.at[i, 0, rows], at.at_z(d))
            wzs[i, 0] = total.astype(BF)
            wzs[i, 0, rows] = plus(total[i * 32:i * 32 + 32], wzr[i, 0, rows]).astype(BF)
        else:
            links.wait(("w", d, s - 1), wzr.at[i, s - 1], at.at_z(d))
            wzs[i, s - 1] = plus(total, wzr[i, s - 1]).astype(BF)
        links.send(("w", d, s), wzs.at[i, s - 1], wzr.at[i, s], at.at_z(d))

    def send_dq():
        dqh[...] = (qacc[...] * SCALE).T.astype(BF).reshape(4, 128, HD)
        scatter_heads("dq", lambda t: dqh.at[(j + t) % 4], head(dq, 0))

    def finish():
        for name, out in (("dq", dq), ("dk", dk), ("dv", dv)):
            await_heads(name, out.at[:, three_heads])
        own["proj"].wait()
        own["wg"].wait()
        links.drain()

    tasks = {
        "K0": k0, "V0": v0, "Q0": q0, "W0": w0, "WY0": wy0, "OG0": og0, "RA": ring_start,
        "R": ring, "W": wstep, "WY": wy, "FY": wforward, "S": wshare, "OG": ogstep, "OL": oglast,
        "SC": scores, "WE": weigh, "HG": head_grad, "GH": send_grad, "FIN": finish_attention,
        "DEL": deltas, "B": backward, "Z": zsend, "ZF": zfinal, "PX": project, "XF": xfirst,
        "XS": xsecond, "XE": xfinal, "ATT": await_attended, "WG": weight_grad, "Y1": yfirst,
        "Y2": ysecond, "Y3": yfinal, "DQ": send_dq, "END": finish,
    }
    for name, *numbers in ORDER:
        tasks[name](*numbers)
    assert len(links.slots) == RECEIVES, len(links.slots)


def hand_over_kernel(*refs):
    for i in range(5):
        refs[5 + i][...] = refs[i][...]


def hand_over(*arrays):
    return pl.pallas_call(
        hand_over_kernel,
        out_shape=tuple(jax.ShapeDtypeStruct(a.shape, a.dtype) for a in arrays),
        in_specs=vmem(5),
        out_specs=tuple(vmem(5)),
        name="hand_over",
    )(*arrays)


def on_device(queries, key_rows, value_rows, out_weight, out_grad, block_offsets):
    heads = jax.ShapeDtypeStruct((128, 512), BF)
    proj, dq, dk, dv, wg = pl.pallas_call(
        kernel,
        out_shape=(
            jax.ShapeDtypeStruct((128, 1024), BF), heads, heads, heads,
            jax.ShapeDtypeStruct((64, 512), F32),
        ),
        in_specs=[pl.BlockSpec(memory_space=pltpu.SMEM)] + any_spec(5),
        out_specs=tuple(any_spec(5)),
        scratch_shapes=[
            pltpu.VMEM((4, 128, HD), BF),
            pltpu.VMEM((2, 8, 4, 128, HD), BF),
            pltpu.VMEM((2, 8, 2, 2, 64, 512), BF),
            pltpu.VMEM((4, 128, 1024), BF),
            pltpu.VMEM((4, 128, HD), BF),
            pltpu.VMEM((4, 128, HD), BF),
            pltpu.VMEM((128, 512), BF),
            pltpu.VMEM((128, 512), BF),
            pltpu.VMEM((4, 128, HD), BF),
            pltpu.VMEM((2, 8, 4, 128, HD), BF),
            pltpu.VMEM((4, 128, 1024), BF),
            pltpu.VMEM((2, 8, 2, 2, 64, 512), BF),
            pltpu.VMEM((2, 2, 4, 4, 128, HD), BF),
            pltpu.VMEM((2, 2, 3, 4, 128, HD), BF),
            pltpu.VMEM((2, 4, 128, HD), BF),
            pltpu.VMEM((2, 64, 1024), BF),
            pltpu.VMEM((2, 128, 1024), BF),
            pltpu.VMEM((2, 128, 1024), BF),
            pltpu.VMEM((128, 1024), BF),
            pltpu.VMEM((2, 8, 2, 64, 512), BF),
            pltpu.VMEM((2, 8, 2, 64, 512), BF),
            pltpu.VMEM((8, 2, 32, 512), BF),
            pltpu.VMEM((8, 2, 64, 512), BF),
            pltpu.VMEM((64, 512), BF),
            pltpu.VMEM((2, 4, 64, 512), BF),
            pltpu.VMEM((2, 3, 64, 512), BF),
            pltpu.VMEM((64, 512), F32),
            pltpu.VMEM((HD, 512), F32),
            pltpu.VMEM((8, 512), F32),
            pltpu.VMEM((8, 512), F32),
            pltpu.VMEM((2, 512, 512), F32),
            pltpu.VMEM((2, 512, 512), BF),
            pltpu.VMEM((128, 512), F32),
            pltpu.VMEM((1, 512), F32),
            pltpu.VMEM((1, 512), F32),
            pltpu.VMEM((1, 512), jnp.int32),
            pltpu.VMEM((HD, 512), F32),
            pltpu.SemaphoreType.DMA((SENDS,)),
            pltpu.SemaphoreType.DMA((RECEIVES,)),
            pltpu.SemaphoreType.DMA((12,)),
        ],
        compiler_params=pltpu.CompilerParams(
            collective_id=0, has_side_effects=True, vmem_limit_bytes=62 << 20),
        name="whole",
    )(block_offsets, queries[0], key_rows[0], value_rows[0], out_weight, out_grad[0])
    proj, dq, dk, dv, wg = hand_over(proj, dq, dk, dv, wg)
    return proj[None], dq[None], dk[None], dv[None], wg


def solution(mesh):
    tokens = P("dp", "ctx", "mp")
    features = P(("dp", "ctx"), "mp")
    return jax.shard_map(
        on_device,
        mesh=mesh,
        in_specs=(tokens, tokens, tokens, features, tokens, P("dp", None)),
        out_specs=(tokens, tokens, tokens, tokens, features),
        check_vma=False,
    )
```

```python
import jax
import jax.numpy as jnp
from jax import lax
from jax.experimental import pallas as pl
from jax.experimental.pallas import tpu as pltpu
from jax.sharding import PartitionSpec as P

HD = 128
MASKED = -1e30
MESH = pl.DeviceIdType.MESH
BF = jnp.bfloat16
F32 = jnp.float32
PHASES = ((-1, 1), (-2, 2), (-3, 3), (4,))


class Place:
    def __init__(self):
        self.dp = lax.axis_index("dp")
        self.ctx = lax.axis_index("ctx")
        self.mp = lax.axis_index("mp")
        self.z = self.ctx // 4
        self.j = self.ctx % 4
        self.yhi = self.j // 2
        self.core = self.j % 2
        self.y = self.yhi * 2 + self.dp

    def plane(self, off):
        return (self.z + 8 + off) % 8

    def yblock(self, off):
        y = (self.y + 4 + off) % 4
        return y % 2, y // 2

    def at_z(self, off):
        return {"ctx": self.plane(off) * 4 + self.j}

    def at_y(self, off):
        dp, yhi = self.yblock(off)
        return {"dp": dp, "ctx": self.z * 4 + yhi * 2 + self.core}

    def at_x(self, off):
        return {"mp": (self.mp + 4 + off) % 4}

    def at_j(self, off):
        return {"ctx": self.z * 4 + (self.j + 4 + off) % 4}

    def sibling(self):
        return {"ctx": self.ctx + 1 - 2 * self.core}


def greet(devices):
    barrier = pltpu.get_barrier_semaphore()
    for device in devices:
        pl.semaphore_signal(barrier, inc=1, device_id=device, device_id_type=MESH)
    pl.semaphore_wait(barrier, len(devices))


class Links:
    def __init__(self, send_sems, recv_sems):
        self.send_sems, self.recv_sems = send_sems, recv_sems
        self.slots = {}
        self.leaving = [None] * SENDS
        self.count = 0

    def copy(self, name, src, dst, device, sender):
        i = self.slots.setdefault(name, len(self.slots))
        return pltpu.make_async_remote_copy(
            src_ref=src, dst_ref=dst, send_sem=self.send_sems.at[sender],
            recv_sem=self.recv_sems.at[i], device_id=device, device_id_type=MESH)

    def send(self, name, src, dst, device):
        i = self.count % SENDS
        self.count += 1
        if self.leaving[i] is not None:
            self.leaving[i].wait_send()
        self.leaving[i] = self.copy(name, src, dst, device, i)
        self.leaving[i].start()

    def wait(self, name, dst, device):
        self.copy(name, dst, dst, device, 0).wait_recv()

    def drain(self):
        for copy in self.leaving:
            copy.wait_send()


def vmem(n):
    return [pl.BlockSpec(memory_space=pltpu.VMEM)] * n


def any_spec(n):
    return [pl.BlockSpec(memory_space=pl.ANY)] * n


GROUPS = ((4,), (3, -3), (2, -2), (1, -1), (0,))
LOG2E = 1.4426950408889634
SCALE = HD ** -0.5
SCALE2 = SCALE * LOG2E
NT = (((1,), (1,)), ((), ()))
TN = (((0,), (0,)), ((), ()))
SIDES = ((0, 1), (1, -1))
SENDS = 32
RECEIVES = 121
ORDER = (
    ("K0",), ("W0",), ("V0",), ("RS", 0, 1), ("RO", 0, -1),
    ("WY0",), ("Q0",), ("RO", 1, 1), ("RO", 0, 1), ("RO", 1, -1),
    ("RS", 0, -1), ("W", 0, 1), ("RS", 1, -1), ("W", 0, -1), ("WY", 1),
    ("RA", 0, 1), ("OG0",), ("RA", 1, -1), ("WY", -1), ("RS", 1, 1),
    ("RA", 0, -1), ("W", 1, 1), ("WY", -2), ("W", 1, -1), ("WY", 2),
    ("RA", 1, 1), ("R", 0, 0, 1), ("FY", 0, -1), ("R", 1, 0, -1), ("W", 2, 1),
    ("WY", -3), ("W", 2, -1), ("WY", 3), ("FY", -1, -1), ("FY", -2, -1),
    ("R", 1, 0, 1), ("FY", -2, 1), ("SC", 0), ("FY", 0, 1), ("FY", -1, 1),
    ("WE", 0), ("R", 0, 0, -1), ("SC", 1), ("FY", 1, -1), ("R", 1, 1, -1),
    ("W", 3, 1), ("W", 3, -1), ("R", 0, 1, 1), ("WY", 4), ("OG", -1),
    ("OG", 1), ("FY", 3, 1), ("FY", 3, -1), ("S", -2), ("FY", 1, 1),
    ("S", 0), ("FY", -3, 1), ("R", 1, 1, 1), ("FY", -3, -1), ("FY", 2, 1),
    ("FY", 2, -1), ("R", 0, 1, -1), ("WE", 1), ("SC", 2), ("FY", 4, 1),
    ("FY", 4, -1), ("S", -1), ("WE", 2), ("S", 3), ("R", 0, 2, 1),
    ("S", -3), ("S", 1), ("OL",), ("HG", -2), ("HG", -1),
    ("R", 1, 2, -1), ("S", 2), ("HG", 0), ("S", 4), ("HG", 3),
    ("HG", -3), ("HG", 1), ("HG", 2), ("HG", 4), ("GH",),
    ("R", 0, 2, -1), ("SC", 3), ("R", 1, 2, 1), ("WE", 3), ("R", 0, 3, 1),
    ("SC", 4), ("R", 1, 3, -1), ("WE", 4), ("FIN",), ("DEL",),
    ("BH", 0), ("ZH", 0, 1), ("ZH", 0, -1), ("BH", 1), ("ZH", 1, 1),
    ("ZH", 1, -1), ("B", -3), ("B", 3), ("Z", 1, 1, 1), ("Z", 0, 1, -1),
    ("ATT",), ("WG", -3), ("WG", 1), ("WG", 4), ("WG", 3),
    ("WG", 2), ("B", 2), ("Y1", -3), ("Z", 1, 1, -1), ("Z", 0, 1, 1),
    ("Y1", 4), ("Y1", 3), ("Y1", 2), ("Y1", 1), ("B", -2),
    ("Z", 0, 2, -1), ("Z", 1, 2, 1), ("Y2", -3, 1), ("Y2", -3, -1), ("WG", -2),
    ("Y2", 4, -1), ("PX", 2), ("XF",), ("Y2", 4, 1), ("WG", -1),
    ("WG", 0), ("Z", 0, 2, 1), ("Z", 1, 2, -1), ("Y2", 2, -1), ("Y1", -2),
    ("Y2", 2, 1), ("Y2", 3, -1), ("Y2", 1, -1), ("B", 1), ("Y2", 3, 1),
    ("Y1", -1), ("Y3", 4), ("Z", 1, 3, 1), ("Y1", 0), ("Y2", 1, 1),
    ("B", -1), ("Z", 1, 3, -1), ("Y2", -2, 1), ("PX", 1), ("PX", -1),
    ("XS", 1), ("Y2", -2, -1), ("Y3", 3), ("Y3", -3), ("XS", -1),
    ("Y2", -1, 1), ("Z", 0, 3, -1), ("Z", 0, 3, 1), ("Y2", -1, -1), ("B", 0),
    ("DQ",), ("Y2", 0, -1), ("Y3", 2), ("ZF", 1), ("Y2", 0, 1),
    ("Y3", -2), ("ZF", 0), ("Y3", 1), ("Y3", -1), ("PX", 0),
    ("XE",), ("Y3", 0), ("END",),
)


def dot(a, b, dims=(((1,), (0,)), ((), ()))):
    return lax.dot_general(a, b, dims, preferred_element_type=F32)


def plus(*terms):
    total = terms[0].astype(F32)
    for term in terms[1:]:
        total = total + term.astype(F32)
    return total


def kernel(offsets, q, k, v, w, og, proj, dq, dk, dv, wg,
           qh, kv, wf, ogf, doh, atth, ghs, att_tok, dqh, dkv, px, wgp,
           zr, zs, zfin, xr0, xs, xr1, projs, sibr, wsum, yr0, yr1, wyb, wzr, wzs, wgs,
           acc, top, norm, sc, pb, gacc, lse, delta, posq, qacc,
           send_sems, recv_sems, local_sems):
    at = Place()
    z, j, core, mp = at.z, at.j, at.core, at.mp
    greet([at.at_j(1), at.at_j(2), at.at_j(3), at.at_z(1), at.at_z(-1),
           at.at_y(1), at.at_y(-1), at.at_x(1), at.at_x(-1)])
    links = Links(send_sems, recv_sems)

    def head(ref, off):
        return ref.at[:, pl.ds(pl.multiple_of((j + 4 + off) % 4 * HD, HD), HD)]

    def wblock(zoff, yoff, half=None):
        dp, yhi = at.yblock(yoff)
        ref = wf.at[dp, at.plane(zoff), yhi, core]
        return ref if half is None else ref.at[pl.ds(half * 32, 32)]

    own = {}

    def keep(name, src, dst):
        own[name] = pltpu.make_async_copy(src, dst, local_sems.at[len(own)])
        own[name].start()

    def scatter_heads(name, blocks, dst):
        for t in (1, 2, 3):
            links.send(name, blocks(t), dst, at.at_j(t))
        keep(name, blocks(0), dst)

    def scatter_kv(a, ref):
        dst = kv.at[a, z, j]
        for c in (0, 1):
            to = 2 - 2 * at.yhi + c
            links.send(("kv", a), head(ref, to - j), dst, {"ctx": z * 4 + to})
        links.send(("kvs", a), head(ref, 1 - 2 * core), dst, at.sibling())
        keep("kv"[a], head(ref, 0), dst)

    def await_heads(name, three):
        links.wait(name, three, at.at_j(1))
        own[name].wait()

    three_blocks = pl.ds(0, 3)
    three_heads = pl.ds(0, 3 * HD)

    def k0():
        scatter_kv(0, k)

    def v0():
        scatter_kv(1, v)

    def q0():
        scatter_heads("q", lambda t: head(q, t), qh.at[j])

    def w0():
        keep("w", w, wblock(0, 0))
        for d in (1, -1):
            links.send(("wz", d, 0), w, wblock(0, 0), at.at_z(d))

    def wy0():
        for d in (1, -1):
            links.send(("wy", 0, d), w, wblock(0, 0), at.at_y(d))

    def og0():
        for d in (1, -1):
            links.send(("og", d, 0), og, ogf.at[mp], at.at_x(d))
        keep("og", og, ogf.at[mp])

    met = set()

    def first(*names):
        fresh = names not in met
        met.add(names)
        return fresh

    def ring_own(a, d):
        links.send(("z", a, d, 0), head((k, v)[a], 0), kv.at[a, z, j], at.at_z(d))

    def ring_sibling(a, d):
        block = kv.at[a, z, j + 1 - 2 * core]
        if first("sibling", a):
            links.wait(("kvs", a), block, at.sibling())
        links.send(("z", a, d, 0), block, block, at.at_z(d))

    def ring_start(a, d):
        pair = kv.at[a, z, pl.ds(2 - 2 * at.yhi, 2)]
        if first("pair", a):
            links.wait(("kv", a), pair, at.at_j(2))
            own["kv"[a]].wait()
        links.send(("z", a, d, 0), pair, pair, at.at_z(d))

    def ring(a, s, d):
        i = (1 - d) // 2
        chunk = kv.at[a, at.plane(-d * (1 + s))]
        links.wait(("z", a, d, s), chunk, at.at_z(d))
        if s < 2 or (s == 2 and a == i):
            links.send(("z", a, d, s + 1), chunk, chunk, at.at_z(d))

    def wstep(s, d):
        i = (1 - d) // 2
        block = wblock(-d * (1 + s), 0) if s < 3 else wblock(4, 0, i)
        links.wait(("wz", d, s), block, at.at_z(d))
        if s < 2:
            links.send(("wz", d, s + 1), block, block, at.at_z(d))
        elif s == 2:
            half = wblock(-d * 3, 0, i)
            links.send(("wz", d, 3), half, half, at.at_z(d))

    def wy(off):
        for d in (1, -1):
            links.send(("wy", off, d), wblock(off, 0), wblock(off, 0), at.at_y(d))

    def wforward(off, d):
        i = (1 - d) // 2
        links.wait(("wy", off, d), wblock(off, -d), at.at_y(d))
        links.send(("wyh", off), wblock(off, -d, i), wblock(off, -d, i), at.at_y(d))

    def wshare(off):
        if off == 0:
            own["w"].wait()
        links.wait(("wyh", off), wblock(off, 2), at.at_y(1))
        for dp in (0, 1):
            ref = wf.at[dp, at.plane(off), :, core]
            links.send(("sib", off), ref, ref, at.sibling())

    def ogstep(d):
        slot = ogf.at[(mp + 4 - d) % 4]
        links.wait(("og", d, 0), slot, at.at_x(d))
        half = slot.at[pl.ds((1 - d) // 2 * 64, 64)]
        links.send("ogh", half, half, at.at_x(d))

    def oglast():
        own["og"].wait()
        links.wait("ogh", ogf.at[(mp + 2) % 4], at.at_x(1))

    row_in = lax.broadcasted_iota(jnp.int32, (128, 512), 0)

    def allowed(plane, start=0, blocks=4):
        return jnp.concatenate(
            [row_in <= posq[...] - offsets[0, plane * 4 + start + i] * 128 for i in range(blocks)],
            axis=0)

    def fold(op, rows):
        return op(rows.reshape(64, 8, 512), axis=0)

    def begin():
        lane = lax.broadcasted_iota(jnp.int32, (1, 512), 1)
        place = lane % 128
        for i in range(4):
            place = place + jnp.where(lane // 128 == i, offsets[0, z * 4 + i] * 128, 0)
        posq[...] = place
        acc[...] = jnp.zeros_like(acc)
        gacc[...] = jnp.zeros_like(gacc)
        qacc[...] = jnp.zeros_like(qacc)
        norm[...] = jnp.zeros_like(norm)
        top[...] = jnp.full_like(top, MASKED)

    def planes(n):
        return (n,) if n in (0, 4) else (-n, n)

    def scores(n):
        if n == 0:
            begin()
            await_heads("q", qh.at[three_blocks])
        qs = qh[...].reshape(512, HD)
        best = top[...]
        for i, off in enumerate(planes(n)):
            plane = at.plane(off)
            s = dot(kv[0, plane].reshape(512, HD), qs, NT) * SCALE2
            s = jnp.where(allowed(plane), s, MASKED)
            sc[i] = s
            best = jnp.maximum(best, fold(jnp.max, s))
        m = jnp.max(best, axis=0, keepdims=True)
        alpha = jnp.exp2(top[0:1] - m)
        top[...] = jnp.broadcast_to(m, (8, 512))
        total = norm[...] * alpha
        for i, off in enumerate(planes(n)):
            p = jnp.exp2(sc[i] - m)
            pb[i] = p.astype(BF)
            total = total + fold(jnp.sum, p)
        norm[...] = total
        acc[...] = acc[...] * alpha

    def weigh(n):
        for i, off in enumerate(planes(n)):
            acc[...] += dot(kv[1, at.plane(off)].reshape(512, HD), pb[i], TN)

    def og_cols(dp, plane):
        cols = pl.ds(pl.multiple_of(plane % 4 * 256, 256), 256)
        return ogf[dp * 2 + plane // 4, :, cols]

    def head_grad(off):
        plane = at.plane(off)
        links.wait(("sib", off), wf.at[:, plane, :, 1 - core], at.sibling())
        gacc[...] += sum(
            dot(og_cols(dp, plane), wf[dp, plane].reshape(256, 512)) for dp in (0, 1))

    def send_grad():
        ghs[...] = gacc[...].astype(BF)
        scatter_heads("g", lambda t: head(ghs, t), doh.at[j])

    def finish_attention():
        total = jnp.sum(norm[...], axis=0, keepdims=True)
        atth[...] = (acc[...] / total).T.astype(BF).reshape(4, 128, HD)
        lse[...] = top[0:1] + jnp.log2(total)
        scatter_heads("a", lambda t: atth.at[(j + t) % 4], head(att_tok, 0))

    def deltas():
        await_heads("g", doh.at[three_blocks])
        products = (doh[...].astype(F32) * atth[...].astype(F32)).reshape(512, HD)
        delta[...] = jnp.sum(products.T, axis=0, keepdims=True)

    def backward_rows(off, first_block, blocks):
        plane = at.plane(off)
        some = pl.ds(first_block, blocks)
        qs = qh[...].reshape(512, HD)
        do = doh[...].reshape(512, HD)
        ks = kv[0, plane, some].reshape(blocks * 128, HD)
        vs = kv[1, plane, some].reshape(blocks * 128, HD)
        s = dot(ks, qs, NT) * SCALE2
        p = jnp.where(allowed(plane, first_block, blocks), jnp.exp2(s - lse[...]), 0.0)
        ds = (p * (dot(vs, do, NT) - delta[...])).astype(BF)
        dkv[1, plane, some] = dot(p.astype(BF), do).astype(BF).reshape(blocks, 128, HD)
        dkv[0, plane, some] = (dot(ds, qs) * SCALE).astype(BF).reshape(blocks, 128, HD)
        qacc[...] += dot(ks, ds, TN)

    def backward(off):
        backward_rows(off, 0, 4)

    def backward_half(h):
        backward_rows(4, h * 2, 2)

    def zhalf(h, d):
        i = (1 - d) // 2
        half = pl.ds(h * 2, 2)
        links.send(("rz", i, d, 0), dkv.at[i, at.plane(4), half], zr.at[i, i, 0, half], at.at_z(d))

    def zsend(a, s, d):
        i = (1 - d) // 2
        p = at.plane(d * (4 - s))
        if s == 1 and a != i:
            src = dkv.at[a, p]
        else:
            links.wait(("rz", a, d, s - 1), zr.at[a, i, s - 1], at.at_z(d))
            zs[a, i, s - 1] = plus(dkv[a, p], zr[a, i, s - 1]).astype(BF)
            src = zs.at[a, i, s - 1]
        links.send(("rz", a, d, s) if s < 3 else ("rz", a, 3), src, zr.at[a, i, s], at.at_z(d))

    def zfinal(a):
        links.wait(("rz", a, 3), zr.at[a, :, 3], at.at_z(1))
        zfin[a] = plus(dkv[a, z], zr[a, 0, 3], zr[a, 1, 3]).astype(BF)
        scatter_heads(("dk", "dv")[a], lambda t: zfin.at[a, (j + t) % 4], head((dk, dv)[a], 0))

    def project(off):
        x = (mp + 4 + off) % 4
        rows = wf[x // 2, pl.ds(pl.multiple_of(x % 2 * 4, 4), 4)].reshape(1024, 512)
        px[x] = dot(att_tok[...], rows, NT).astype(BF)

    def xfirst():
        for i, d in SIDES:
            links.send(("x", d, 0), px.at[(mp + 2) % 4, pl.ds(i * 64, 64)], xr0.at[i], at.at_x(d))

    def xsecond(d):
        i = (1 - d) // 2
        chunk = (mp + 4 + d) % 4
        links.wait(("x", d, 0), xr0.at[i], at.at_x(d))
        xs[i, pl.ds(i * 64, 64)] = plus(px[chunk, pl.ds(i * 64, 64)], xr0[i]).astype(BF)
        xs[i, pl.ds(64 - i * 64, 64)] = px[chunk, pl.ds(64 - i * 64, 64)]
        links.send("xlast", xs.at[i], xr1.at[i], at.at_x(d))

    def xfinal():
        links.wait("xlast", xr1, at.at_x(1))
        projs[...] = plus(px[mp], xr1[0], xr1[1]).astype(BF)
        keep("proj", projs, proj)

    def await_attended():
        await_heads("a", att_tok.at[:, three_heads])

    def weight_grad(off):
        p = at.plane(off)
        for dp in (0, 1):
            part = dot(og_cols(dp, p), att_tok[...], TN).astype(BF)
            wgp[dp, p] = part.reshape(2, 2, 64, 512)
            links.send(("wsib", off), wgp.at[dp, p, :, 1 - core], sibr.at[dp, p], at.sibling())

    def yfirst(off):
        p = at.plane(off)
        links.wait(("wsib", off), sibr.at[:, p], at.sibling())
        for dp in (0, 1):
            for yhi in (0, 1):
                wsum[dp, p, yhi] = plus(wgp[dp, p, yhi, core], sibr[dp, p, yhi]).astype(BF)
        dp, yhi = at.yblock(2)
        for i, d in SIDES:
            links.send(("y", off, d, 0), wsum.at[dp, p, yhi, pl.ds(i * 32, 32)], yr0.at[p, i], at.at_y(d))

    def ysecond(off, d):
        p = at.plane(off)
        i = (1 - d) // 2
        dp, yhi = at.yblock(d)
        links.wait(("y", off, d, 0), yr0.at[p, i], at.at_y(d))
        rows = pl.ds(i * 32, 32)
        wsum[dp, p, yhi, rows] = plus(wsum[dp, p, yhi, rows], yr0[p, i]).astype(BF)
        links.send(("ylast", off), wsum.at[dp, p, yhi], yr1.at[p, i], at.at_y(d))

    def yfinal(off):
        p = at.plane(off)
        links.wait(("ylast", off), yr1.at[p], at.at_y(1))
        total = plus(wsum[at.dp, p, at.yhi], yr1[p, 0], yr1[p, 1])
        if off == 0:
            links.wait("wlast", wzr.at[:, 3], at.at_z(1))
            wgs[...] = plus(total, wzr[0, 3], wzr[1, 3])
            keep("wg", wgs, wg)
            return
        if off == 4:
            wyb[...] = total.astype(BF)
            for i, d in SIDES:
                rows = pl.ds(i * 32, 32)
                links.send(("w", d, 0), wyb.at[rows], wzr.at[i, 0, rows], at.at_z(d))
            return
        d = 1 if off > 0 else -1
        i = (1 - d) // 2
        s = 4 - abs(off)
        if s == 1:
            rows = pl.ds(i * 32, 32)
            links.wait(("w", d, 0), wzr.at[i, 0, rows], at.at_z(d))
            wzs[i, 0] = total.astype(BF)
            wzs[i, 0, rows] = plus(total[i * 32:i * 32 + 32], wzr[i, 0, rows]).astype(BF)
        else:
            links.wait(("w", d, s - 1), wzr.at[i, s - 1], at.at_z(d))
            wzs[i, s - 1] = plus(total, wzr[i, s - 1]).astype(BF)
        links.send(("w", d, s) if s < 3 else "wlast", wzs.at[i, s - 1], wzr.at[i, s], at.at_z(d))

    def send_dq():
        dqh[...] = (qacc[...] * SCALE).T.astype(BF).reshape(4, 128, HD)
        scatter_heads("dq", lambda t: dqh.at[(j + t) % 4], head(dq, 0))

    def finish():
        for name, out in (("dq", dq), ("dk", dk), ("dv", dv)):
            await_heads(name, out.at[:, three_heads])
        own["proj"].wait()
        own["wg"].wait()
        links.drain()

    tasks = {
        "K0": k0, "V0": v0, "Q0": q0, "W0": w0, "WY0": wy0, "OG0": og0, "RA": ring_start, "RO": ring_own, "RS": ring_sibling, "BH": backward_half, "ZH": zhalf,
        "R": ring, "W": wstep, "WY": wy, "FY": wforward, "S": wshare, "OG": ogstep, "OL": oglast,
        "SC": scores, "WE": weigh, "HG": head_grad, "GH": send_grad, "FIN": finish_attention,
        "DEL": deltas, "B": backward, "Z": zsend, "ZF": zfinal, "PX": project, "XF": xfirst,
        "XS": xsecond, "XE": xfinal, "ATT": await_attended, "WG": weight_grad, "Y1": yfirst,
        "Y2": ysecond, "Y3": yfinal, "DQ": send_dq, "END": finish,
    }
    for name, *numbers in ORDER:
        tasks[name](*numbers)
    assert len(links.slots) == RECEIVES, len(links.slots)


def hand_over_kernel(*refs):
    for i in range(5):
        refs[5 + i][...] = refs[i][...]


def hand_over(*arrays):
    return pl.pallas_call(
        hand_over_kernel,
        out_shape=tuple(jax.ShapeDtypeStruct(a.shape, a.dtype) for a in arrays),
        in_specs=vmem(5),
        out_specs=tuple(vmem(5)),
        name="hand_over",
    )(*arrays)


def on_device(queries, key_rows, value_rows, out_weight, out_grad, block_offsets):
    heads = jax.ShapeDtypeStruct((128, 512), BF)
    proj, dq, dk, dv, wg = pl.pallas_call(
        kernel,
        out_shape=(
            jax.ShapeDtypeStruct((128, 1024), BF), heads, heads, heads,
            jax.ShapeDtypeStruct((64, 512), F32),
        ),
        in_specs=[pl.BlockSpec(memory_space=pltpu.SMEM)] + any_spec(5),
        out_specs=tuple(any_spec(5)),
        scratch_shapes=[
            pltpu.VMEM((4, 128, HD), BF),
            pltpu.VMEM((2, 8, 4, 128, HD), BF),
            pltpu.VMEM((2, 8, 2, 2, 64, 512), BF),
            pltpu.VMEM((4, 128, 1024), BF),
            pltpu.VMEM((4, 128, HD), BF),
            pltpu.VMEM((4, 128, HD), BF),
            pltpu.VMEM((128, 512), BF),
            pltpu.VMEM((128, 512), BF),
            pltpu.VMEM((4, 128, HD), BF),
            pltpu.VMEM((2, 8, 4, 128, HD), BF),
            pltpu.VMEM((4, 128, 1024), BF),
            pltpu.VMEM((2, 8, 2, 2, 64, 512), BF),
            pltpu.VMEM((2, 2, 4, 4, 128, HD), BF),
            pltpu.VMEM((2, 2, 3, 4, 128, HD), BF),
            pltpu.VMEM((2, 4, 128, HD), BF),
            pltpu.VMEM((2, 64, 1024), BF),
            pltpu.VMEM((2, 128, 1024), BF),
            pltpu.VMEM((2, 128, 1024), BF),
            pltpu.VMEM((128, 1024), BF),
            pltpu.VMEM((2, 8, 2, 64, 512), BF),
            pltpu.VMEM((2, 8, 2, 64, 512), BF),
            pltpu.VMEM((8, 2, 32, 512), BF),
            pltpu.VMEM((8, 2, 64, 512), BF),
            pltpu.VMEM((64, 512), BF),
            pltpu.VMEM((2, 4, 64, 512), BF),
            pltpu.VMEM((2, 3, 64, 512), BF),
            pltpu.VMEM((64, 512), F32),
            pltpu.VMEM((HD, 512), F32),
            pltpu.VMEM((8, 512), F32),
            pltpu.VMEM((8, 512), F32),
            pltpu.VMEM((2, 512, 512), F32),
            pltpu.VMEM((2, 512, 512), BF),
            pltpu.VMEM((128, 512), F32),
            pltpu.VMEM((1, 512), F32),
            pltpu.VMEM((1, 512), F32),
            pltpu.VMEM((1, 512), jnp.int32),
            pltpu.VMEM((HD, 512), F32),
            pltpu.SemaphoreType.DMA((SENDS,)),
            pltpu.SemaphoreType.DMA((RECEIVES,)),
            pltpu.SemaphoreType.DMA((12,)),
        ],
        compiler_params=pltpu.CompilerParams(
            collective_id=0, has_side_effects=True, vmem_limit_bytes=62 << 20),
        name="whole",
    )(block_offsets, queries[0], key_rows[0], value_rows[0], out_weight, out_grad[0])
    proj, dq, dk, dv, wg = hand_over(proj, dq, dk, dv, wg)
    return proj[None], dq[None], dk[None], dv[None], wg


def solution(mesh):
    tokens = P("dp", "ctx", "mp")
    features = P(("dp", "ctx"), "mp")
    return jax.shard_map(
        on_device,
        mesh=mesh,
        in_specs=(tokens, tokens, tokens, features, tokens, P("dp", None)),
        out_specs=(tokens, tokens, tokens, tokens, features),
        check_vma=False,
    )
```

```python
import jax
import jax.numpy as jnp
from jax import lax
from jax.experimental import pallas as pl
from jax.experimental.pallas import tpu as pltpu
from jax.sharding import PartitionSpec as P

HD = 128
MASKED = -1e30
MESH = pl.DeviceIdType.MESH
BF = jnp.bfloat16
F32 = jnp.float32
PHASES = ((-1, 1), (-2, 2), (-3, 3), (4,))


class Place:
    def __init__(self):
        self.dp = lax.axis_index("dp")
        self.ctx = lax.axis_index("ctx")
        self.mp = lax.axis_index("mp")
        self.z = self.ctx // 4
        self.j = self.ctx % 4
        self.yhi = self.j // 2
        self.core = self.j % 2
        self.y = self.yhi * 2 + self.dp

    def plane(self, off):
        return (self.z + 8 + off) % 8

    def yblock(self, off):
        y = (self.y + 4 + off) % 4
        return y % 2, y // 2

    def at_z(self, off):
        return {"ctx": self.plane(off) * 4 + self.j}

    def at_y(self, off):
        dp, yhi = self.yblock(off)
        return {"dp": dp, "ctx": self.z * 4 + yhi * 2 + self.core}

    def at_x(self, off):
        return {"mp": (self.mp + 4 + off) % 4}

    def at_j(self, off):
        return {"ctx": self.z * 4 + (self.j + 4 + off) % 4}

    def sibling(self):
        return {"ctx": self.ctx + 1 - 2 * self.core}


def greet(devices):
    barrier = pltpu.get_barrier_semaphore()
    for device in devices:
        pl.semaphore_signal(barrier, inc=1, device_id=device, device_id_type=MESH)
    pl.semaphore_wait(barrier, len(devices))


class Links:
    def __init__(self, send_sems, recv_sems):
        self.send_sems, self.recv_sems = send_sems, recv_sems
        self.slots = {}
        self.leaving = [None] * SENDS
        self.count = 0

    def copy(self, name, src, dst, device, sender):
        i = self.slots.setdefault(name, len(self.slots))
        return pltpu.make_async_remote_copy(
            src_ref=src, dst_ref=dst, send_sem=self.send_sems.at[sender],
            recv_sem=self.recv_sems.at[i], device_id=device, device_id_type=MESH)

    def send(self, name, src, dst, device):
        i = self.count % SENDS
        self.count += 1
        if self.leaving[i] is not None:
            self.leaving[i].wait_send()
        self.leaving[i] = self.copy(name, src, dst, device, i)
        self.leaving[i].start()

    def wait(self, name, dst, device):
        self.copy(name, dst, dst, device, 0).wait_recv()

    def drain(self):
        for copy in self.leaving:
            copy.wait_send()


def vmem(n):
    return [pl.BlockSpec(memory_space=pltpu.VMEM)] * n


def any_spec(n):
    return [pl.BlockSpec(memory_space=pl.ANY)] * n


GROUPS = ((4,), (3, -3), (2, -2), (1, -1), (0,))
LOG2E = 1.4426950408889634
SCALE = HD ** -0.5
SCALE2 = SCALE * LOG2E
NT = (((1,), (1,)), ((), ()))
TN = (((0,), (0,)), ((), ()))
SIDES = ((0, 1), (1, -1))
SENDS = 32
RECEIVES = 121
ORDER = (
    ("K0",), ("W0",), ("V0",), ("RS", 1, 1), ("Q0",),
    ("RS", 0, -1), ("RS", 1, -1), ("RO", 1, -1), ("RO", 1, 1), ("RS", 0, 1),
    ("OG0",), ("W", 0, 1), ("WY", -1), ("WY0",), ("RO", 0, -1),
    ("RA", 0, 1), ("RO", 0, 1), ("W", 0, -1), ("WY", 1), ("RA", 1, -1),
    ("RA", 0, -1), ("W", 1, 1), ("WY", -2), ("RA", 1, 1), ("W", 1, -1),
    ("WY", 2), ("R", 0, 0, 1), ("R", 1, 0, -1), ("FY", 0, -1), ("W", 2, 1),
    ("WY", -3), ("FY", -2, 1), ("FY", -2, -1), ("R", 1, 0, 1), ("W", 2, -1),
    ("WY", 3), ("SC", 0), ("WE", 0), ("OG", 1), ("FY", -1, 1),
    ("FY", 0, 1), ("R", 0, 0, -1), ("FY", -1, -1), ("W", 3, 1), ("W", 3, -1),
    ("WY", 4), ("R", 0, 1, 1), ("R", 1, 1, -1), ("FY", -3, 1), ("FY", 3, 1),
    ("FY", -3, -1), ("FY", 2, -1), ("OG", -1), ("SC", 1), ("WE", 1),
    ("FY", 2, 1), ("FY", 3, -1), ("FY", 1, 1), ("FY", 1, -1), ("S", -2),
    ("R", 1, 1, 1), ("R", 0, 1, -1), ("FY", 4, 1), ("S", 0), ("FY", 4, -1),
    ("S", -1), ("S", -3), ("SC", 2), ("R", 0, 2, 1), ("S", 2),
    ("S", 3), ("R", 1, 2, -1), ("S", 1), ("OL",), ("HG", 0),
    ("S", 4), ("HG", -3), ("HG", -2), ("HG", -1), ("HG", 2),
    ("HG", 3), ("HG", 1), ("HG", 4), ("GH",), ("WE", 2),
    ("R", 0, 2, -1), ("SC", 3), ("R", 1, 2, 1), ("WE", 3), ("R", 1, 3, -1),
    ("R", 0, 3, 1), ("SC", 4), ("WE", 4), ("FIN",), ("DEL",),
    ("BH", 0), ("ZH", 0, 1), ("ZH", 0, -1), ("BH", 1), ("ZH", 1, -1),
    ("ZH", 1, 1), ("B", -3), ("Z", 0, 1, -1), ("B", 3), ("Z", 1, 1, 1),
    ("ATT",), ("WG", 4), ("WG", -3), ("WG", 2), ("WG", 3),
    ("PX", 2), ("WG", 1), ("XF",), ("WG", 0), ("WG", -1),
    ("Y1", 4), ("Z", 1, 1, -1), ("Z", 0, 1, 1), ("Y1", -3), ("WG", -2),
    ("Y1", 1), ("Y1", 3), ("B", 2), ("Y2", 4, -1), ("Y2", 4, 1),
    ("Z", 1, 2, 1), ("B", -2), ("Z", 0, 2, -1), ("Y1", 2), ("Y1", -2),
    ("Y1", -1), ("Z", 0, 2, 1), ("Y1", 0), ("Y3", 4), ("Y2", -3, -1),
    ("Y2", -3, 1), ("Z", 1, 2, -1), ("B", 1), ("Z", 1, 3, 1), ("Y2", 3, 1),
    ("Y2", 3, -1), ("Y2", -2, -1), ("Y2", -2, 1), ("B", -1), ("Z", 0, 3, -1),
    ("Y2", 2, -1), ("PX", -1), ("Y2", 2, 1), ("PX", 1), ("XS", 1),
    ("Y3", -3), ("Y2", 1, -1), ("Y2", 0, -1), ("Y3", 3), ("Y2", -1, -1),
    ("Z", 0, 3, 1), ("Z", 1, 3, -1), ("Y2", 0, 1), ("PX", 0), ("Y2", 1, 1),
    ("XS", -1), ("B", 0), ("DQ",), ("Y3", 2), ("Y2", -1, 1),
    ("Y3", -2), ("ZF", 0), ("ZF", 1), ("Y3", 1), ("Y3", -1),
    ("XE",), ("Y3", 0), ("END",),
)


def dot(a, b, dims=(((1,), (0,)), ((), ()))):
    return lax.dot_general(a, b, dims, preferred_element_type=F32)


def plus(*terms):
    total = terms[0].astype(F32)
    for term in terms[1:]:
        total = total + term.astype(F32)
    return total


def kernel(offsets, q, k, v, w, og, proj, dq, dk, dv, wg,
           qh, kv, wf, ogf, doh, atth, ghs, att_tok, dqh, dkv, px, wgp,
           zr, zs, zfin, xr0, xs, xr1, projs, sibr, wsum, yr0, yr1, wyb, wzr, wzs, wgs,
           acc, top, norm, sc, pb, gacc, lse, delta, posq, qacc,
           send_sems, recv_sems, local_sems):
    at = Place()
    z, j, core, mp = at.z, at.j, at.core, at.mp
    greet([at.at_j(1), at.at_j(2), at.at_j(3), at.at_z(1), at.at_z(-1),
           at.at_y(1), at.at_y(-1), at.at_x(1), at.at_x(-1)])
    links = Links(send_sems, recv_sems)

    def head(ref, off):
        return ref.at[:, pl.ds(pl.multiple_of((j + 4 + off) % 4 * HD, HD), HD)]

    def wblock(zoff, yoff, half=None):
        dp, yhi = at.yblock(yoff)
        ref = wf.at[dp, at.plane(zoff), yhi, core]
        return ref if half is None else ref.at[pl.ds(half * 32, 32)]

    own = {}

    def keep(name, src, dst):
        own[name] = pltpu.make_async_copy(src, dst, local_sems.at[len(own)])
        own[name].start()

    def scatter_heads(name, blocks, dst):
        for t in (1, 2, 3):
            links.send(name, blocks(t), dst, at.at_j(t))
        keep(name, blocks(0), dst)

    def scatter_kv(a, ref):
        dst = kv.at[a, z, j]
        for c in (0, 1):
            to = 2 - 2 * at.yhi + c
            links.send(("kv", a), head(ref, to - j), dst, {"ctx": z * 4 + to})
        links.send(("kvs", a), head(ref, 1 - 2 * core), dst, at.sibling())
        keep("kv"[a], head(ref, 0), dst)

    def await_heads(name, three):
        links.wait(name, three, at.at_j(1))
        own[name].wait()

    three_blocks = pl.ds(0, 3)
    three_heads = pl.ds(0, 3 * HD)

    def k0():
        scatter_kv(0, k)

    def v0():
        scatter_kv(1, v)

    def q0():
        scatter_heads("q", lambda t: head(q, t), qh.at[j])

    def w0():
        keep("w", w, wblock(0, 0))
        for d in (1, -1):
            links.send(("wz", d, 0), w, wblock(0, 0), at.at_z(d))

    def wy0():
        for d in (1, -1):
            links.send(("wy", 0, d), w, wblock(0, 0), at.at_y(d))

    def og0():
        for d in (1, -1):
            links.send(("og", d, 0), og, ogf.at[mp], at.at_x(d))
        keep("og", og, ogf.at[mp])

    met = set()

    def first(*names):
        fresh = names not in met
        met.add(names)
        return fresh

    def ring_own(a, d):
        links.send(("z", a, d, 0), head((k, v)[a], 0), kv.at[a, z, j], at.at_z(d))

    def ring_sibling(a, d):
        block = kv.at[a, z, j + 1 - 2 * core]
        if first("sibling", a):
            links.wait(("kvs", a), block, at.sibling())
        links.send(("z", a, d, 0), block, block, at.at_z(d))

    def ring_start(a, d):
        pair = kv.at[a, z, pl.ds(2 - 2 * at.yhi, 2)]
        if first("pair", a):
            links.wait(("kv", a), pair, at.at_j(2))
            own["kv"[a]].wait()
        links.send(("z", a, d, 0), pair, pair, at.at_z(d))

    def ring(a, s, d):
        i = (1 - d) // 2
        chunk = kv.at[a, at.plane(-d * (1 + s))]
        links.wait(("z", a, d, s), chunk, at.at_z(d))
        if s < 2 or (s == 2 and a == i):
            links.send(("z", a, d, s + 1), chunk, chunk, at.at_z(d))

    def wstep(s, d):
        i = (1 - d) // 2
        block = wblock(-d * (1 + s), 0) if s < 3 else wblock(4, 0, i)
        links.wait(("wz", d, s), block, at.at_z(d))
        if s < 2:
            links.send(("wz", d, s + 1), block, block, at.at_z(d))
        elif s == 2:
            half = wblock(-d * 3, 0, i)
            links.send(("wz", d, 3), half, half, at.at_z(d))

    def wy(off):
        for d in (1, -1):
            links.send(("wy", off, d), wblock(off, 0), wblock(off, 0), at.at_y(d))

    def wforward(off, d):
        i = (1 - d) // 2
        links.wait(("wy", off, d), wblock(off, -d), at.at_y(d))
        links.send(("wyh", off), wblock(off, -d, i), wblock(off, -d, i), at.at_y(d))

    def wshare(off):
        if off == 0:
            own["w"].wait()
        links.wait(("wyh", off), wblock(off, 2), at.at_y(1))
        for dp in (0, 1):
            ref = wf.at[dp, at.plane(off), :, core]
            links.send(("sib", off), ref, ref, at.sibling())

    def ogstep(d):
        slot = ogf.at[(mp + 4 - d) % 4]
        links.wait(("og", d, 0), slot, at.at_x(d))
        half = slot.at[pl.ds((1 - d) // 2 * 64, 64)]
        links.send("ogh", half, half, at.at_x(d))

    def oglast():
        own["og"].wait()
        links.wait("ogh", ogf.at[(mp + 2) % 4], at.at_x(1))

    row_in = lax.broadcasted_iota(jnp.int32, (128, 512), 0)

    def allowed(plane, start=0, blocks=4):
        return jnp.concatenate(
            [row_in <= posq[...] - offsets[0, plane * 4 + start + i] * 128 for i in range(blocks)],
            axis=0)

    def fold(op, rows):
        return op(rows.reshape(64, 8, 512), axis=0)

    def begin():
        lane = lax.broadcasted_iota(jnp.int32, (1, 512), 1)
        place = lane % 128
        for i in range(4):
            place = place + jnp.where(lane // 128 == i, offsets[0, z * 4 + i] * 128, 0)
        posq[...] = place
        acc[...] = jnp.zeros_like(acc)
        gacc[...] = jnp.zeros_like(gacc)
        qacc[...] = jnp.zeros_like(qacc)
        norm[...] = jnp.zeros_like(norm)
        top[...] = jnp.full_like(top, MASKED)

    def planes(n):
        return (n,) if n in (0, 4) else (-n, n)

    def scores(n):
        if n == 0:
            begin()
            await_heads("q", qh.at[three_blocks])
        qs = qh[...].reshape(512, HD)
        best = top[...]
        for i, off in enumerate(planes(n)):
            plane = at.plane(off)
            s = dot(kv[0, plane].reshape(512, HD), qs, NT) * SCALE2
            s = jnp.where(allowed(plane), s, MASKED)
            sc[i] = s
            best = jnp.maximum(best, fold(jnp.max, s))
        m = jnp.max(best, axis=0, keepdims=True)
        alpha = jnp.exp2(top[0:1] - m)
        top[...] = jnp.broadcast_to(m, (8, 512))
        total = norm[...] * alpha
        for i, off in enumerate(planes(n)):
            p = jnp.exp2(sc[i] - m)
            pb[i] = p.astype(BF)
            total = total + fold(jnp.sum, p)
        norm[...] = total
        acc[...] = acc[...] * alpha

    def weigh(n):
        for i, off in enumerate(planes(n)):
            acc[...] += dot(kv[1, at.plane(off)].reshape(512, HD), pb[i], TN)

    def og_cols(dp, plane):
        cols = pl.ds(pl.multiple_of(plane % 4 * 256, 256), 256)
        return ogf[dp * 2 + plane // 4, :, cols]

    def head_grad(off):
        plane = at.plane(off)
        links.wait(("sib", off), wf.at[:, plane, :, 1 - core], at.sibling())
        gacc[...] += sum(
            dot(og_cols(dp, plane), wf[dp, plane].reshape(256, 512)) for dp in (0, 1))

    def send_grad():
        ghs[...] = gacc[...].astype(BF)
        scatter_heads("g", lambda t: head(ghs, t), doh.at[j])

    def finish_attention():
        total = jnp.sum(norm[...], axis=0, keepdims=True)
        atth[...] = (acc[...] / total).T.astype(BF).reshape(4, 128, HD)
        lse[...] = top[0:1] + jnp.log2(total)
        scatter_heads("a", lambda t: atth.at[(j + t) % 4], head(att_tok, 0))

    def deltas():
        await_heads("g", doh.at[three_blocks])
        products = (doh[...].astype(F32) * atth[...].astype(F32)).reshape(512, HD)
        delta[...] = jnp.sum(products.T, axis=0, keepdims=True)

    def backward_rows(off, first_block, blocks):
        plane = at.plane(off)
        some = pl.ds(first_block, blocks)
        qs = qh[...].reshape(512, HD)
        do = doh[...].reshape(512, HD)
        ks = kv[0, plane, some].reshape(blocks * 128, HD)
        vs = kv[1, plane, some].reshape(blocks * 128, HD)
        s = dot(ks, qs, NT) * SCALE2
        p = jnp.where(allowed(plane, first_block, blocks), jnp.exp2(s - lse[...]), 0.0)
        ds = (p * (dot(vs, do, NT) - delta[...])).astype(BF)
        dkv[1, plane, some] = dot(p.astype(BF), do).astype(BF).reshape(blocks, 128, HD)
        dkv[0, plane, some] = (dot(ds, qs) * SCALE).astype(BF).reshape(blocks, 128, HD)
        qacc[...] += dot(ks, ds, TN)

    def backward(off):
        backward_rows(off, 0, 4)

    def backward_half(h):
        backward_rows(4, h * 2, 2)

    def zhalf(h, d):
        i = (1 - d) // 2
        half = pl.ds(h * 2, 2)
        links.send(("rz", i, d, 0), dkv.at[i, at.plane(4), half], zr.at[i, i, 0, half], at.at_z(d))

    def zsend(a, s, d):
        i = (1 - d) // 2
        p = at.plane(d * (4 - s))
        if s == 1 and a != i:
            src = dkv.at[a, p]
        else:
            links.wait(("rz", a, d, s - 1), zr.at[a, i, s - 1], at.at_z(d))
            zs[a, i, s - 1] = plus(dkv[a, p], zr[a, i, s - 1]).astype(BF)
            src = zs.at[a, i, s - 1]
        links.send(("rz", a, d, s) if s < 3 else ("rz", a, 3), src, zr.at[a, i, s], at.at_z(d))

    def zfinal(a):
        links.wait(("rz", a, 3), zr.at[a, :, 3], at.at_z(1))
        zfin[a] = plus(dkv[a, z], zr[a, 0, 3], zr[a, 1, 3]).astype(BF)
        scatter_heads(("dk", "dv")[a], lambda t: zfin.at[a, (j + t) % 4], head((dk, dv)[a], 0))

    def project(off):
        x = (mp + 4 + off) % 4
        rows = wf[x // 2, pl.ds(pl.multiple_of(x % 2 * 4, 4), 4)].reshape(1024, 512)
        px[x] = dot(att_tok[...], rows, NT).astype(BF)

    def xfirst():
        for i, d in SIDES:
            links.send(("x", d, 0), px.at[(mp + 2) % 4, pl.ds(i * 64, 64)], xr0.at[i], at.at_x(d))

    def xsecond(d):
        i = (1 - d) // 2
        chunk = (mp + 4 + d) % 4
        links.wait(("x", d, 0), xr0.at[i], at.at_x(d))
        xs[i, pl.ds(i * 64, 64)] = plus(px[chunk, pl.ds(i * 64, 64)], xr0[i]).astype(BF)
        xs[i, pl.ds(64 - i * 64, 64)] = px[chunk, pl.ds(64 - i * 64, 64)]
        links.send("xlast", xs.at[i], xr1.at[i], at.at_x(d))

    def xfinal():
        links.wait("xlast", xr1, at.at_x(1))
        projs[...] = plus(px[mp], xr1[0], xr1[1]).astype(BF)
        keep("proj", projs, proj)

    def await_attended():
        await_heads("a", att_tok.at[:, three_heads])

    def weight_grad(off):
        p = at.plane(off)
        for dp in (0, 1):
            part = dot(og_cols(dp, p), att_tok[...], TN).astype(BF)
            wgp[dp, p] = part.reshape(2, 2, 64, 512)
            links.send(("wsib", off), wgp.at[dp, p, :, 1 - core], sibr.at[dp, p], at.sibling())

    def yfirst(off):
        p = at.plane(off)
        links.wait(("wsib", off), sibr.at[:, p], at.sibling())
        for dp in (0, 1):
            for yhi in (0, 1):
                wsum[dp, p, yhi] = plus(wgp[dp, p, yhi, core], sibr[dp, p, yhi]).astype(BF)
        dp, yhi = at.yblock(2)
        for i, d in SIDES:
            links.send(("y", off, d, 0), wsum.at[dp, p, yhi, pl.ds(i * 32, 32)], yr0.at[p, i], at.at_y(d))

    def ysecond(off, d):
        p = at.plane(off)
        i = (1 - d) // 2
        dp, yhi = at.yblock(d)
        links.wait(("y", off, d, 0), yr0.at[p, i], at.at_y(d))
        rows = pl.ds(i * 32, 32)
        wsum[dp, p, yhi, rows] = plus(wsum[dp, p, yhi, rows], yr0[p, i]).astype(BF)
        links.send(("ylast", off), wsum.at[dp, p, yhi], yr1.at[p, i], at.at_y(d))

    def yfinal(off):
        p = at.plane(off)
        links.wait(("ylast", off), yr1.at[p], at.at_y(1))
        total = plus(wsum[at.dp, p, at.yhi], yr1[p, 0], yr1[p, 1])
        if off == 0:
            links.wait("wlast", wzr.at[:, 3], at.at_z(1))
            wgs[...] = plus(total, wzr[0, 3], wzr[1, 3])
            keep("wg", wgs, wg)
            return
        if off == 4:
            wyb[...] = total.astype(BF)
            for i, d in SIDES:
                rows = pl.ds(i * 32, 32)
                links.send(("w", d, 0), wyb.at[rows], wzr.at[i, 0, rows], at.at_z(d))
            return
        d = 1 if off > 0 else -1
        i = (1 - d) // 2
        s = 4 - abs(off)
        if s == 1:
            rows = pl.ds(i * 32, 32)
            links.wait(("w", d, 0), wzr.at[i, 0, rows], at.at_z(d))
            wzs[i, 0] = total.astype(BF)
            wzs[i, 0, rows] = plus(total[i * 32:i * 32 + 32], wzr[i, 0, rows]).astype(BF)
        else:
            links.wait(("w", d, s - 1), wzr.at[i, s - 1], at.at_z(d))
            wzs[i, s - 1] = plus(total, wzr[i, s - 1]).astype(BF)
        links.send(("w", d, s) if s < 3 else "wlast", wzs.at[i, s - 1], wzr.at[i, s], at.at_z(d))

    def send_dq():
        dqh[...] = (qacc[...] * SCALE).T.astype(BF).reshape(4, 128, HD)
        scatter_heads("dq", lambda t: dqh.at[(j + t) % 4], head(dq, 0))

    def finish():
        for name, out in (("dq", dq), ("dk", dk), ("dv", dv)):
            await_heads(name, out.at[:, three_heads])
        own["proj"].wait()
        own["wg"].wait()
        links.drain()

    tasks = {
        "K0": k0, "V0": v0, "Q0": q0, "W0": w0, "WY0": wy0, "OG0": og0, "RA": ring_start, "RO": ring_own, "RS": ring_sibling, "BH": backward_half, "ZH": zhalf,
        "R": ring, "W": wstep, "WY": wy, "FY": wforward, "S": wshare, "OG": ogstep, "OL": oglast,
        "SC": scores, "WE": weigh, "HG": head_grad, "GH": send_grad, "FIN": finish_attention,
        "DEL": deltas, "B": backward, "Z": zsend, "ZF": zfinal, "PX": project, "XF": xfirst,
        "XS": xsecond, "XE": xfinal, "ATT": await_attended, "WG": weight_grad, "Y1": yfirst,
        "Y2": ysecond, "Y3": yfinal, "DQ": send_dq, "END": finish,
    }
    for name, *numbers in ORDER:
        tasks[name](*numbers)
    assert len(links.slots) == RECEIVES, len(links.slots)


def hand_over_kernel(*refs):
    for i in range(5):
        refs[5 + i][...] = refs[i][...]


def hand_over(*arrays):
    return pl.pallas_call(
        hand_over_kernel,
        out_shape=tuple(jax.ShapeDtypeStruct(a.shape, a.dtype) for a in arrays),
        in_specs=vmem(5),
        out_specs=tuple(vmem(5)),
        name="hand_over",
    )(*arrays)


def on_device(queries, key_rows, value_rows, out_weight, out_grad, block_offsets):
    heads = jax.ShapeDtypeStruct((128, 512), BF)
    proj, dq, dk, dv, wg = pl.pallas_call(
        kernel,
        out_shape=(
            jax.ShapeDtypeStruct((128, 1024), BF), heads, heads, heads,
            jax.ShapeDtypeStruct((64, 512), F32),
        ),
        in_specs=[pl.BlockSpec(memory_space=pltpu.SMEM)] + any_spec(5),
        out_specs=tuple(any_spec(5)),
        scratch_shapes=[
            pltpu.VMEM((4, 128, HD), BF),
            pltpu.VMEM((2, 8, 4, 128, HD), BF),
            pltpu.VMEM((2, 8, 2, 2, 64, 512), BF),
            pltpu.VMEM((4, 128, 1024), BF),
            pltpu.VMEM((4, 128, HD), BF),
            pltpu.VMEM((4, 128, HD), BF),
            pltpu.VMEM((128, 512), BF),
            pltpu.VMEM((128, 512), BF),
            pltpu.VMEM((4, 128, HD), BF),
            pltpu.VMEM((2, 8, 4, 128, HD), BF),
            pltpu.VMEM((4, 128, 1024), BF),
            pltpu.VMEM((2, 8, 2, 2, 64, 512), BF),
            pltpu.VMEM((2, 2, 4, 4, 128, HD), BF),
            pltpu.VMEM((2, 2, 3, 4, 128, HD), BF),
            pltpu.VMEM((2, 4, 128, HD), BF),
            pltpu.VMEM((2, 64, 1024), BF),
            pltpu.VMEM((2, 128, 1024), BF),
            pltpu.VMEM((2, 128, 1024), BF),
            pltpu.VMEM((128, 1024), BF),
            pltpu.VMEM((2, 8, 2, 64, 512), BF),
            pltpu.VMEM((2, 8, 2, 64, 512), BF),
            pltpu.VMEM((8, 2, 32, 512), BF),
            pltpu.VMEM((8, 2, 64, 512), BF),
            pltpu.VMEM((64, 512), BF),
            pltpu.VMEM((2, 4, 64, 512), BF),
            pltpu.VMEM((2, 3, 64, 512), BF),
            pltpu.VMEM((64, 512), F32),
            pltpu.VMEM((HD, 512), F32),
            pltpu.VMEM((8, 512), F32),
            pltpu.VMEM((8, 512), F32),
            pltpu.VMEM((2, 512, 512), F32),
            pltpu.VMEM((2, 512, 512), BF),
            pltpu.VMEM((128, 512), F32),
            pltpu.VMEM((1, 512), F32),
            pltpu.VMEM((1, 512), F32),
            pltpu.VMEM((1, 512), jnp.int32),
            pltpu.VMEM((HD, 512), F32),
            pltpu.SemaphoreType.DMA((SENDS,)),
            pltpu.SemaphoreType.DMA((RECEIVES,)),
            pltpu.SemaphoreType.DMA((12,)),
        ],
        compiler_params=pltpu.CompilerParams(
            collective_id=0, has_side_effects=True, vmem_limit_bytes=62 << 20),
        name="whole",
    )(block_offsets, queries[0], key_rows[0], value_rows[0], out_weight, out_grad[0])
    proj, dq, dk, dv, wg = hand_over(proj, dq, dk, dv, wg)
    return proj[None], dq[None], dk[None], dv[None], wg


def solution(mesh):
    tokens = P("dp", "ctx", "mp")
    features = P(("dp", "ctx"), "mp")
    return jax.shard_map(
        on_device,
        mesh=mesh,
        in_specs=(tokens, tokens, tokens, features, tokens, P("dp", None)),
        out_specs=(tokens, tokens, tokens, tokens, features),
        check_vma=False,
    )
```
